256 devices in a mesh: segment: 4 (over z_hi), dp: 64 (over y, z_lo, x, core).
Axes of the slice: x: 4, y: 4, z: 8 (z_hi: 4, z_lo: 2; z = z_hi * 2 + z_lo), core: 2. Of those that a mesh axis runs over, the one named last changes fastest.
Arguments:
- layer_inputs: bfloat16 [4, 3072, 4096], P(None, 'dp'), may hold values from -6 to 6
- top_cotangent: bfloat16 [4, 3072, 4096], P(None, 'dp'), may hold values from -1.5 to 1.5
- norm_gains: float32 [4, 4096], P('segment'), may hold values from 0.5 to 1.5
- down_weight: bfloat16 [4, 4096, 512], P('segment'), may hold values from -0.09375 to 0.09375
- up_weight: bfloat16 [4, 512, 4096], P('segment'), may hold values from -0.25 to 0.25
Outputs:
- grad_gain: float32 [4, 4096], P('segment')
- grad_down: float32 [4, 4096, 512], P('segment', 'dp')
- grad_up: float32 [4, 512, 4096], P('segment', 'dp')
The draws below stay inside these ranges and needn't reach their ends.
All inputs are finite; a program needn't handle non-finite values.
Results may differ from the reference program's by a relative error of at most 0.014.
Values may be sent and summed in bfloat16 or wider, within the bound.
No kernel may reach another device: no remote copies, remote signals or barrier semaphores. Data moves between devices by JAX's collectives and lax.ppermute only.
A program may use at most 128 MiB of HBM per device.

```python
import jax
import jax.numpy as jnp
from jax import lax

D = 4096
KVW = 512
MICRO = 4
SECTIONS = 4
TOKENS = 3072


def spiked(array, stream_key, source, target, blocks, factor):
    owner, partner = [(jnp.arange(array.shape[axis_at]) // (array.shape[axis_at] // blocks)).reshape([-1 if axis == axis_at else 1 for axis in range(array.ndim)]) for axis_at in (source, target)]
    chosen = jax.random.permutation(stream_key, blocks)[partner]
    strong = (owner == chosen) | (owner == (partner + blocks // 2) % blocks)
    return jnp.where(strong, factor * array, array)


def steps_of(key, extent, shards, low, high):
    loudness, own = 1.0, jax.random.fold_in(key, 6)
    for axis_at, shards_of in shards:
        steps = jnp.exp(jax.random.uniform(jax.random.fold_in(own, axis_at), (shards_of,), jnp.float32, low / len(shards), high / len(shards)))
        loudness = loudness * jnp.repeat(steps, extent[axis_at] // shards_of).reshape([-1 if axis == axis_at else 1 for axis in range(len(extent))])
    return loudness


def scatter_about(stream_key, shape, scale, most, shards=(), dtype=jnp.bfloat16):
    drawn = jax.random.normal(stream_key, shape, jnp.float32) * scale
    if len(shards) > 0:
        drawn = steps_of(stream_key, shape, shards, -0.22, 0.18) * drawn
    return jnp.clip(drawn, min=-most, max=most).astype(dtype)


def bell_draw_with(own_key, dims, scale, limit, pieces, heavy, kind=jnp.bfloat16):
    drawn = scale * jax.random.normal(own_key, dims, jnp.float32)
    if pieces:
        drawn = drawn * steps_of(own_key, dims, pieces, -0.22, 0.18)
    return jnp.clip(spiked(drawn, jax.random.fold_in(own_key, 3), *heavy), -limit, limit).astype(kind)


def setup_inputs(seed: int = 0) -> dict:
    keys = jax.random.split(jax.random.key(seed), 6)
    return {
        "layer_inputs": scatter_about(keys[0], (MICRO, TOKENS, D), 1.0, 6.0, ((1, 64),)),
        "top_cotangent": bell_draw_with(keys[1], (MICRO, TOKENS, D), (4.0 / (MICRO * TOKENS) ** 0.5), 1.5, ((1, 64),), (1, 2, 64, 4.0)),
        "norm_gains": jnp.clip(1.0 + 0.1 * jax.random.normal(keys[2], (SECTIONS, D), jnp.float32), 0.5, 1.5),
        "down_weight": scatter_about(keys[3], (SECTIONS, D, KVW), D ** -0.5, 0.09375, ((0, 4),)),
        "up_weight": scatter_about(keys[4], (SECTIONS, KVW, D), KVW ** -0.5, 0.25, ((0, 4),)),
    }


eps = 1e-05

def forward_section(activation, gain_row, down_matrix, up_matrix):
    widened = activation.astype(jnp.float32)
    inverse_rms = lax.rsqrt(lax.optimization_barrier(jnp.mean(widened * widened, axis=-1, keepdims=True)) + eps)
    normed = (widened * inverse_rms * gain_row).astype(jnp.bfloat16)
    projected = jnp.dot(normed, down_matrix, preferred_element_type=jnp.float32)
    hidden = jax.nn.silu(projected).astype(jnp.bfloat16)
    result = (widened + jnp.dot(hidden, up_matrix, preferred_element_type=jnp.float32)).astype(jnp.bfloat16)
    return (result, inverse_rms, normed, projected, hidden)

def backward_section(activation, inverse_rms, projected, upstream, gain_row, down_matrix, up_matrix):
    contract_last = (((1,), (1,)), ((), ()))
    hidden_grad = lax.dot_general(upstream, up_matrix, contract_last, preferred_element_type=jnp.float32)
    logistic = jax.nn.sigmoid(projected)
    silu_slope = logistic * (1.0 + projected * (1.0 - logistic))
    value_grad = (hidden_grad * silu_slope).astype(jnp.bfloat16)
    normed_grad = lax.dot_general(value_grad, down_matrix, contract_last, preferred_element_type=jnp.float32)
    unit_rows = activation.astype(jnp.float32) * inverse_rms
    gain_term = lax.optimization_barrier(jnp.sum(normed_grad * unit_rows, axis=0))
    scaled_grad = normed_grad * gain_row
    norm_grad = inverse_rms * (scaled_grad - unit_rows * lax.optimization_barrier(jnp.mean(scaled_grad * unit_rows, axis=-1, keepdims=True)))
    passed = (upstream.astype(jnp.float32) + norm_grad).astype(jnp.bfloat16)
    return (passed, value_grad, gain_term)

def rows_product(left, right):
    return lax.dot_general(left, right, (((0,), (0,)), ((), ())), preferred_element_type=jnp.float32)

def reference(layer_inputs, top_cotangent, norm_gains, down_weight, up_weight):
    down_totals = [jnp.zeros((D, KVW), jnp.float32) for section in range(SECTIONS)]
    up_totals = [jnp.zeros((KVW, D), jnp.float32) for section in range(SECTIONS)]
    gain_totals = [jnp.zeros((D,), jnp.float32) for section in range(SECTIONS)]
    for micro in range(MICRO):
        current = layer_inputs[micro]
        saved = []
        for section in range(SECTIONS):
            result, inverse_rms, normed, projected, hidden = forward_section(current, norm_gains[section], down_weight[section], up_weight[section])
            saved.append((current, inverse_rms, normed, projected, hidden))
            current = result
        upstream = top_cotangent[micro]
        for section in range(SECTIONS - 1, -1, -1):
            activation, inverse_rms, normed, projected, hidden = saved[section]
            up_totals[section] = up_totals[section] + rows_product(hidden, upstream)
            passed, value_grad, gain_term = backward_section(activation, inverse_rms, projected, upstream, norm_gains[section], down_weight[section], up_weight[section])
            down_totals[section] = down_totals[section] + rows_product(normed, value_grad)
            gain_totals[section] = gain_totals[section] + gain_term
            upstream = passed
    return (jnp.stack(gain_totals), jnp.stack(down_totals), jnp.stack(up_totals))
```

```python
import jax
import jax.numpy as jnp
from jax import lax
from jax.sharding import Mesh
from jax.sharding import PartitionSpec as P

eps = 1e-05
bf16 = jnp.bfloat16
f32 = jnp.float32
GROUPS = ("row", "half", "col", "core")


def shift(block, axis, distance):
    count = lax.axis_size(axis)
    return lax.ppermute(block, axis, [(j, (j + distance) % count) for j in range(count)])


def swap(block, axis):
    return lax.ppermute(block, axis, [(0, 1), (1, 0)])


def dot(left, right, dims=((1,), (0,))):
    return lax.dot_general(left, right, (dims, ((), ())), preferred_element_type=f32)


def in_order(blocks, place):
    stacked = jnp.stack(blocks)
    return lax.dynamic_slice_in_dim(
        jnp.concatenate([stacked, stacked]), (4 - place) % 4, 4, axis=0
    )


def gather4(block, axis):
    return [block] + [shift(block, axis, 4 - t) for t in (1, 2, 3)]


def pick(array, index, size, axis):
    return lax.dynamic_slice_in_dim(array, index * size, size, axis=axis)


def split_lanes(column):
    high = lax.reduce_precision(column, 8, 7)
    low = column - high
    rows = column.shape[0]
    return jnp.concatenate(
        [jnp.broadcast_to(high, (rows, 64)), jnp.broadcast_to(low, (rows, 64))], axis=1
    ).astype(bf16)


def join_lanes(lanes):
    wide = lanes.astype(f32)
    return wide[:, 0:1] + wide[:, 64:65]


def col_slices(rows):
    return [
        jnp.concatenate([rows[:, b * 512 + t * 128 : b * 512 + t * 128 + 128] for b in range(8)], 1)
        for t in range(4)
    ]


def col_exchange(rows, col):
    parts = jnp.stack(col_slices(rows))
    blocks = []
    for d in range(4):
        part = lax.dynamic_index_in_dim(parts, (col + d) % 4, 0, keepdims=False)
        blocks.append(part if d == 0 else shift(part, "col", d))
    return jnp.concatenate(blocks, 0)


def col_reduce(partial, extra=None):
    sent = partial.astype(bf16)
    if extra is not None:
        sent = jnp.concatenate([sent, split_lanes(extra)], 1)
    total = partial[:48]
    extra_total = None if extra is None else extra[:48]
    for d in (1, 2, 3):
        got = shift(sent[48 * d : 48 * d + 48], "col", -d)
        total = total + got[:, :512].astype(f32)
        if extra is not None:
            extra_total = extra_total + join_lanes(got[:, 512:])
    return total, extra_total


def col_spread(block):
    return jnp.concatenate([block] + [shift(block, "col", d) for d in (1, 2, 3)], 0)


def slope(v):
    logistic = jax.nn.sigmoid(v)
    return logistic * (1.0 + v * (1.0 - logistic))


def per_device(layer_inputs, top_cotangent, norm_gains, down_weight, up_weight):
    seg = lax.axis_index("segment")
    row = lax.axis_index("row")
    half = lax.axis_index("half")
    col = lax.axis_index("col")
    core = lax.axis_index("core")
    gain = norm_gains[0]
    down = down_weight[0]
    up = up_weight[0]

    rows_in = lax.dynamic_index_in_dim(layer_inputs, seg, 0, keepdims=False)
    rows_top = lax.dynamic_index_in_dim(top_cotangent, seg, 0, keepdims=False)

    scaled_down = (down.astype(f32) * gain[:, None]).astype(bf16)
    first = dot(layer_inputs.reshape(192, 4096), scaled_down).reshape(4, 48, 512).astype(bf16)
    last = (
        dot(top_cotangent.reshape(192, 4096), up, ((1,), (1,))).reshape(4, 48, 512).astype(bf16)
    )
    passed = [first[0]]
    for d in (1, 2, 3):
        sent = jnp.where(seg == 0, first[d], last[d - 1])
        passed.append(lax.ppermute(sent, "segment", [(0, d), (3, d - 1)]))
    passed.append(last[3])
    passed = jnp.stack(passed)
    first_projected = lax.dynamic_index_in_dim(passed, seg, 0, keepdims=False).astype(f32)
    last_hidden_grad = lax.dynamic_index_in_dim(passed, seg + 1, 0, keepdims=False).astype(f32)

    x_rows = [col_exchange(rows_in, col)]

    piece = row * 2 + core
    up_rows = pick(up, piece, 64, 0)
    up_piece = lax.dynamic_index_in_dim(jnp.stack(col_slices(up_rows)), col, 0, keepdims=False)
    up_piece = jnp.concatenate([up_piece[:, :512], up_piece[:, 512:]], 0)
    down_piece = lax.dynamic_slice_in_dim(scaled_down, (piece * 4 + col) * 128, 128, axis=0)
    up_pieces = in_order(gather4(up_piece, "segment"), seg)
    down_pieces = in_order(gather4(down_piece, "segment"), seg)

    def whole(s):
        own = jnp.concatenate([up_pieces[s], down_pieces[s + 1]], 0)
        mine = in_order(gather4(own, "row"), row)
        other = swap(mine, "core")
        both = jnp.stack([jnp.where(core == 0, mine, other), jnp.where(core == 0, other, mine)], 1)
        left = both[:, :, :64].reshape(512, 512)
        right = both[:, :, 64:128].reshape(512, 512)
        return jnp.concatenate([left, right], 1), both[:, :, 128:].reshape(1024, 512)

    ups, downs = [], [None]
    for s in range(3):
        u, w = whole(s)
        ups.append(u)
        downs.append(w)

    top_rows = col_exchange(rows_top, col)

    wide = rows_in.astype(f32)
    inverse_rms = [lax.rsqrt(jnp.mean(wide * wide, axis=-1, keepdims=True) + eps)]
    projected = [inverse_rms[0] * first_projected]
    hidden = []
    for s in range(3):
        hidden.append(col_spread(jax.nn.silu(projected[s]).astype(bf16)))
        x_next = (x_rows[s].astype(f32) + dot(hidden[s], ups[s])).astype(bf16)
        x_rows.append(x_next)
        wide = x_next.astype(f32)
        total, squares = col_reduce(
            dot(x_next, downs[s + 1]), jnp.sum(wide * wide, axis=-1, keepdims=True)
        )
        inverse_rms.append(lax.rsqrt(squares * (1.0 / 4096.0) + eps))
        projected.append(inverse_rms[s + 1] * total)

    reduced = []
    upstream = top_rows
    for s in (3, 2, 1, 0):
        if s == 3:
            hidden_grad = last_hidden_grad
        else:
            hidden_grad, _ = col_reduce(dot(upstream, ups[s], ((1,), (1,))))
        value_grad = hidden_grad * slope(projected[s]) * inverse_rms[s]
        sent = [value_grad.astype(bf16)]
        if s > 0:
            pull = inverse_rms[s] * (
                jnp.sum(value_grad * projected[s], axis=-1, keepdims=True) * (1.0 / 4096.0)
            )
            sent.append(split_lanes(pull))
        if s == 3:
            sent.append(jax.nn.silu(projected[3]).astype(bf16))
        spread = col_spread(jnp.concatenate(sent, 1) if len(sent) > 1 else sent[0])
        value_rows = spread[:, :512]
        if s == 3:
            hidden.append(spread[:, 640:])

        down_kept = dot(x_rows[s], pick(value_rows, core, 256, 1), ((0,), (0,)))
        down_sent = dot(x_rows[s], pick(value_rows, 1 - core, 256, 1), ((0,), (0,)))
        up_kept = dot(hidden[s], pick(upstream, core, 512, 1), ((0,), (0,)))
        up_sent = dot(hidden[s], pick(upstream, 1 - core, 512, 1), ((0,), (0,)))
        down_sum = down_kept + swap(down_sent.astype(bf16), "core").astype(f32)
        up_sum = up_kept + swap(up_sent.astype(bf16), "core").astype(f32)

        def row_part(index):
            part = pick(up_sum, index, 128, 0)
            return jnp.concatenate([pick(down_sum, index, 256, 0), part[:, :256], part[:, 256:]], 0)

        row_sum = row_part(row)
        for d in (1, 2, 3):
            row_sum = row_sum + shift(row_part((row + d) % 4).astype(bf16), "row", d).astype(f32)

        def half_part(index):
            return jnp.concatenate(
                [
                    pick(row_sum[:256], index, 128, 0),
                    pick(row_sum[256:384], index, 64, 0),
                    pick(row_sum[384:], index, 64, 0),
                ],
                0,
            )

        reduced.append(
            half_part(half) + swap(half_part(1 - half).astype(bf16), "half").astype(f32)
        )

        if s > 0:
            upstream = (
                upstream.astype(f32)
                + dot(value_rows, downs[s], ((1,), (1,)))
                - join_lanes(spread[:, 512:640]) * x_rows[s].astype(f32)
            ).astype(bf16)

    reduced = jnp.stack(reduced[::-1])
    whole_sum = lax.dynamic_index_in_dim(reduced, seg, 0, keepdims=False)
    for d in (1, 2, 3):
        part = lax.dynamic_index_in_dim(reduced, (seg + d) % 4, 0, keepdims=False)
        whole_sum = whole_sum + shift(part.astype(bf16), "segment", d).astype(f32)

    down_part = whole_sum[:128]
    up_part = jnp.concatenate([whole_sum[128:192], whole_sum[192:]], 1).reshape(4, 2, 8, 512)
    down_mine = pick(down_part, core, 64, 0)
    down_other = swap(pick(down_part, 1 - core, 64, 0), "core")
    product = jnp.where(
        core == 0,
        jnp.concatenate([down_mine, down_other], 1),
        jnp.concatenate([down_other, down_mine], 1),
    )
    up_mine = lax.dynamic_index_in_dim(up_part, core, 1, keepdims=False)
    up_other = swap(lax.dynamic_index_in_dim(up_part, 1 - core, 1, keepdims=False), "core")
    up_rows = jnp.where(
        core == 0,
        jnp.concatenate([up_mine, up_other], 2),
        jnp.concatenate([up_other, up_mine], 2),
    )
    blocks = [lax.dynamic_index_in_dim(up_rows, col, 0, keepdims=False)]
    for t in (1, 2, 3):
        part = lax.dynamic_index_in_dim(up_rows, (col + 4 - t) % 4, 0, keepdims=False)
        blocks.append(shift(part, "col", 4 - t))
    ordered = in_order(blocks, col)
    up_out = jnp.concatenate(
        [ordered[t, :, b * 128 : b * 128 + 128] for b in range(8) for t in range(4)], 1
    )

    place = ((row * 2 + half) * 4 + col) * 2 + core
    gain_part = jnp.sum(product * pick(down, place, 64, 0).astype(f32), axis=1)
    down_out = product * pick(gain, place, 64, 0)[:, None]

    gain_row = gain_part[None]
    gain_other = swap(gain_row, "core")
    gain_row = jnp.where(
        core == 0,
        jnp.concatenate([gain_row, gain_other], 1),
        jnp.concatenate([gain_other, gain_row], 1),
    )
    gain_row = in_order(gather4(gain_row, "col"), col).reshape(1, 512)
    gain_other = swap(gain_row, "half")
    gain_row = jnp.where(
        half == 0,
        jnp.concatenate([gain_row, gain_other], 1),
        jnp.concatenate([gain_other, gain_row], 1),
    )
    gain_out = in_order(gather4(gain_row, "row"), row).reshape(1, 4096)
    return gain_out, down_out[None], up_out[None]


def solution(mesh):
    fine = Mesh(mesh.devices.reshape(4, 4, 2, 4, 2), ("segment",) + GROUPS)
    return jax.shard_map(
        per_device,
        mesh=fine,
        in_specs=(
            P(None, GROUPS, None),
            P(None, GROUPS, None),
            P("segment", None),
            P("segment", None, None),
            P("segment", None, None),
        ),
        out_specs=(P("segment", None), P("segment", GROUPS, None), P("segment", GROUPS, None)),
        check_vma=False,
    )
```

```python
import jax
import jax.numpy as jnp
from jax import lax
from jax.experimental import pallas as pl
from jax.experimental.pallas import tpu as pltpu
from jax.sharding import Mesh
from jax.sharding import PartitionSpec as P

eps = 1e-05
bf16 = jnp.bfloat16
f32 = jnp.float32
GROUPS = ("row", "half", "col", "core")
VMEM_BYTES = 24 * 1024 * 1024


def shift(block, axis, distance):
    count = lax.axis_size(axis)
    return lax.ppermute(block, axis, [(j, (j + distance) % count) for j in range(count)])


def swap(block, axis):
    return lax.ppermute(block, axis, [(0, 1), (1, 0)])


def dot(left, right, dims=((1,), (0,))):
    return lax.dot_general(left, right, (dims, ((), ())), preferred_element_type=f32)


def rows_product(left, right):
    return dot(left, right, ((0,), (0,)))


def gather4(block, axis):
    return [block] + [shift(block, axis, 4 - t) for t in (1, 2, 3)]


def from_all(block):
    return [block] + [shift(block, "col", d) for d in (1, 2, 3)]


def pick(array, index, size, axis):
    return lax.dynamic_slice_in_dim(array, index * size, size, axis=axis)


def choose(blocks, index):
    return lax.select_n(index.astype(jnp.int32), *blocks)


def after(arrays, first):
    return list(lax.optimization_barrier(tuple(arrays) + tuple(first)))[: len(arrays)]


def two_parts(array):
    high = lax.reduce_precision(array, 8, 7)
    return high.astype(bf16), (array - high).astype(bf16)


def call(kernel, outs, *operands, places=None, scratch=()):
    whole = pl.BlockSpec(memory_space=pltpu.VMEM)
    specs = [whole] * len(operands)
    if places is not None:
        specs = [pl.BlockSpec(memory_space=pltpu.SMEM)] + specs
        operands = (places,) + operands
    return pl.pallas_call(
        kernel,
        out_shape=[jax.ShapeDtypeStruct(shape, dtype) for shape, dtype in outs],
        in_specs=specs,
        out_specs=[whole] * len(outs),
        scratch_shapes=[pltpu.VMEM(shape, dtype) for shape, dtype in scratch],
        compiler_params=pltpu.CompilerParams(vmem_limit_bytes=VMEM_BYTES),
    )(*operands)


def silu_of(v):
    return (v / (1.0 + jnp.exp(-v))).astype(bf16)


def slope(v):
    logistic = 1.0 / (1.0 + jnp.exp(-v))
    return logistic * (1.0 + v * (1.0 - logistic))


def as_lanes(column):
    high = column.astype(bf16).astype(f32)
    lane = lax.broadcasted_iota(jnp.int32, (column.shape[0], 128), 1)
    return jnp.where(lane < 64, high, column - high).astype(bf16)


def of_lanes(block):
    return block[:, :1].astype(f32) + block[:, 64:65].astype(f32)


def prep_kernel(places, x_ref, top_ref, up_ref, p0, p1, p2, p3, piece, rms):
    col = places[1]
    for d, out in enumerate((p0, p1, p2, p3)):
        t = lax.rem(col + d, 4)
        for b in range(8):
            lanes = pl.ds(pl.multiple_of(b * 512 + t * 128, 128), 128)
            out[:48, b * 128 : b * 128 + 128] = x_ref[0, :, lanes]
            out[48:, b * 128 : b * 128 + 128] = top_ref[0, :, lanes]
    for b in range(8):
        lanes = pl.ds(pl.multiple_of(b * 512 + col * 128, 128), 128)
        low = (b // 4) * 128
        piece[low : low + 128, (b % 4) * 128 : (b % 4) * 128 + 128] = up_ref[:, lanes]
    squares = jnp.zeros((48, 1), f32)
    for b in range(4):
        wide = x_ref[0, :, b * 1024 : b * 1024 + 1024].astype(f32)
        squares = squares + jnp.sum(wide * wide, axis=-1, keepdims=True)
    rms[...] = as_lanes(lax.rsqrt(squares * (1.0 / 4096.0) + eps))


def prep(places, layer_inputs, top_cotangent, up):
    rows = pl.BlockSpec((1, 48, 4096), lambda g, p: (p[0], 0, 0))
    shapes = [(96, 1024)] * 4 + [(256, 512), (48, 128)]
    return pl.pallas_call(
        prep_kernel,
        grid_spec=pltpu.PrefetchScalarGridSpec(
            num_scalar_prefetch=1,
            grid=(1,),
            in_specs=[rows, rows, pl.BlockSpec((128, 4096), lambda g, p: (p[2], 0))],
            out_specs=[pl.BlockSpec(shape, lambda g, p: (0, 0)) for shape in shapes],
        ),
        out_shape=[jax.ShapeDtypeStruct(shape, bf16) for shape in shapes],
        compiler_params=pltpu.CompilerParams(vmem_limit_bytes=VMEM_BYTES),
    )(places, layer_inputs, top_cotangent, up)


def grow(places, x_ref, h_ref, mine, other, x_out, sent):
    row, first = places[2], places[3] == 0
    grown = x_ref[...].astype(f32)
    for t in range(4):
        y = lax.rem(row + t, 4)
        h = h_ref[:, pl.ds(pl.multiple_of(y * 128, 128), 128)]
        part = jnp.where(first, mine[t], other[t])
        grown = grown + jnp.concatenate([dot(h, part[:128]), dot(h, part[128:])], 1)
    x_out[...] = grown.astype(bf16)
    wide = x_out[...].astype(f32)
    squares = jnp.sum(wide * wide, axis=-1, keepdims=True)
    total = jnp.zeros((192, 512), f32)
    for t in range(4):
        y = lax.rem(row + t, 4)
        rows = x_out[:, pl.ds(pl.multiple_of(y * 256, 128), 256)]
        total = total + dot(rows, jnp.where(first, other[t], mine[t]))
    sent[:, :512] = total.astype(bf16)
    sent[:, 512:] = as_lanes(squares)


def first_kernel(
    places, b0, b1, b2, b3, x0, x1, x2, x3, mine, other, x_start, top, v, r, h, x_out, sent
):
    for j, (b, x) in enumerate(zip((b0, b1, b2, b3), (x0, x1, x2, x3))):
        rows = slice(48 * j, 48 * j + 48)
        x_start[rows, :] = x[:48]
        top[rows, :] = x[48:]
        inverse_rms = of_lanes(b[:, 512:640])
        block = inverse_rms * b[:, :512].astype(f32)
        v[rows, :] = block
        r[rows, :] = jnp.broadcast_to(inverse_rms, (48, 128))
        h[rows, :] = silu_of(block)
    grow(places, x_start, h, mine, other, x_out, sent)


def summed(refs, total, squares=None):
    own = refs[0]
    for j in range(4):
        rows = slice(48 * j, 48 * j + 48)
        value = own[rows, :512].astype(f32)
        if squares is not None:
            column = of_lanes(own[rows, 512:])
        for d in (1, 2, 3):
            low = 48 * ((j - d) % 4)
            value = value + refs[d][low : low + 48, :512].astype(f32)
            if squares is not None:
                column = column + of_lanes(refs[d][low : low + 48, 512:])
        total[rows, :] = value
        if squares is not None:
            squares[rows, :] = jnp.broadcast_to(column, (48, 128))


def normed(refs, v, r):
    summed(refs, v, r)
    r[...] = lax.rsqrt(r[...] * (1.0 / 4096.0) + eps)
    v[...] = r[:, :1] * v[...]


def forward_kernel(places, p0, p1, p2, p3, x, mine, other, v, r, h, x_out, sent):
    normed((p0, p1, p2, p3), v, r)
    h[...] = silu_of(v[...])
    grow(places, x, h, mine, other, x_out, sent)


def down_gradient(places, q_out, x, mine, other, acc, gain_sum):
    row, first = places[2], places[3] == 0
    for t in range(4):
        y = lax.rem(row + t, 4)
        lanes = pl.ds(pl.multiple_of(y * 256, 128), 256)
        added = dot(q_out[...], jnp.where(first, other[t], mine[t]), ((1,), (1,)))
        gain_sum[:, lanes] = jnp.sum(added * x[:, lanes].astype(f32), axis=0, keepdims=True)
        if acc is not None:
            acc[:, lanes] = acc[:, lanes] + added


def pass_back(places, e, v, r, g, x, mine, other, q_out, g_out, gain_sum, sent, acc):
    row, first = places[2], places[3] == 0
    contract = ((1,), (1,))
    inverse_rms = r[:, :1]
    value_grad = e[...] * slope(v[...]) * inverse_rms
    q_out[...] = value_grad.astype(bf16)
    pull = inverse_rms * (
        jnp.sum(value_grad * v[...], axis=-1, keepdims=True) * (1.0 / 4096.0)
    )
    acc[...] = g[...].astype(f32) - pull * x[...].astype(f32)
    down_gradient(places, q_out, x, mine, other, acc, gain_sum)
    g_out[...] = acc[...].astype(bf16)
    for t in range(4):
        y = lax.rem(row + t, 4)
        part = jnp.where(first, mine[t], other[t])
        product = dot(g_out[:, :512], part[:128], contract) + dot(
            g_out[:, 512:], part[128:], contract
        )
        sent[:, pl.ds(pl.multiple_of(y * 128, 128), 128)] = product.astype(bf16)


def turn_kernel(
    places, p0, p1, p2, p3, b0, b1, b2, b3, g, x, mine, other,
    q_out, g_out, gain_sum, sent, h, acc, e, v, r,
):
    normed((p0, p1, p2, p3), v, r)
    h[...] = silu_of(v[...])
    for j, b in enumerate((b0, b1, b2, b3)):
        e[48 * j : 48 * j + 48, :] = b[:, 640:].astype(f32)
    pass_back(places, e, v, r, g, x, mine, other, q_out, g_out, gain_sum, sent, acc)


def backward_kernel(
    places, p0, p1, p2, p3, v, r, g, x, mine, other, q_out, g_out, gain_sum, sent, acc, e
):
    summed((p0, p1, p2, p3), e)
    pass_back(places, e, v, r, g, x, mine, other, q_out, g_out, gain_sum, sent, acc)


def last_kernel(places, p0, p1, p2, p3, v, r, x, mine, other, q_out, gain_sum, e):
    summed((p0, p1, p2, p3), e)
    q_out[...] = (e[...] * slope(v[...]) * r[:, :1]).astype(bf16)
    down_gradient(places, q_out, x, mine, other, None, gain_sum)


def per_device(layer_inputs, top_cotangent, norm_gains, down_weight, up_weight):
    seg = lax.axis_index("segment")
    row = lax.axis_index("row")
    half = lax.axis_index("half")
    col = lax.axis_index("col")
    core = lax.axis_index("core")
    places = jnp.stack([seg, col, row, core]).astype(jnp.int32)
    gain = norm_gains[0]
    down = down_weight[0]
    up = up_weight[0]

    *parts, up_piece, start_rms = prep(places, layer_inputs, top_cotangent, up)

    down_piece = jnp.concatenate(
        [
            lax.dynamic_slice_in_dim(down, ((row * 2 + b) * 4 + col) * 128, 128, axis=0).astype(f32)
            * lax.dynamic_slice_in_dim(gain, ((row * 2 + b) * 4 + col) * 128, 128, axis=0)[:, None]
            for b in (0, 1)
        ],
        0,
    ).astype(bf16)
    pieces = gather4(jnp.where(core == 0, up_piece, down_piece), "segment")

    scaled = (layer_inputs.astype(f32) * gain).astype(bf16).reshape(192, 4096)
    first = dot(scaled, down).reshape(4, 48, 512).astype(bf16)
    last = dot(top_cotangent.reshape(192, 4096), up, ((1,), (1,))).reshape(4, 48, 512).astype(bf16)
    passed = [first[0]]
    for d in (1, 2, 3):
        sent = jnp.where(seg == 0, first[d], last[d - 1])
        passed.append(lax.ppermute(sent, "segment", [(0, d), (3, d - 1)]))
    passed.append(last[3])
    start = jnp.concatenate(
        [choose(passed[:4], seg), start_rms, choose(passed[1:], seg)], 1
    )
    starts = from_all(start)
    x_blocks = [parts[0]] + [shift(parts[d], "col", d) for d in (1, 2, 3)]

    def weight_blocks(groups):
        own = [choose(pieces, (s + core - seg + 4) % 4) for s in groups]
        return gather4(own[0] if len(own) == 1 else jnp.concatenate(own, 0), "row")

    blocks = [weight_blocks((0,)), weight_blocks((1,)), weight_blocks((2, 3))]

    wide, narrow = ((192, 1024), bf16), ((192, 512), bf16)
    values = [((192, 512), f32), ((192, 128), f32)]
    mine = jnp.stack(blocks[0])
    weights = [(mine, swap(mine, "core"))]
    x_start, top, v, r, h, x_next, sent = call(
        first_kernel,
        [wide, wide, *values, narrow, wide, ((192, 640), bf16)],
        *starts, *x_blocks, *weights[0], places=places,
    )
    x_rows, hidden, saved = [x_start, x_next], [h], [(v, r)]
    for s in (1, 2):
        got = from_all(sent)
        mine = jnp.stack(after(blocks[s], [sent]))
        other = swap(mine, "core")
        if s == 1:
            weights.append((mine, other))
        else:
            weights.append((mine[:, :256], other[:, :256]))
            weights.append((mine[:, 256:], other[:, 256:]))
        v, r, h, x_next, sent = call(
            forward_kernel,
            [*values, narrow, wide, ((192, 640), bf16)],
            *got, x_rows[s], *weights[s], places=places,
        )
        x_rows.append(x_next)
        hidden.append(h)
        saved.append((v, r))
    got = from_all(sent)

    def down_products(s, q):
        kept = rows_product(x_rows[s], pick(q, core, 256, 1))
        return kept, rows_product(x_rows[s], pick(q, 1 - core, 256, 1)).astype(bf16)

    def up_products(s, g):
        kept = rows_product(hidden[s], pick(g, core, 512, 1))
        return kept, rows_product(hidden[s], pick(g, 1 - core, 512, 1)).astype(bf16)

    def fold(product):
        if product.shape[1] == 256:
            return product.reshape(4, 2, 128, 256)
        lanes = product.reshape(4, 2, 64, 512)
        return jnp.concatenate([lanes[..., :256], lanes[..., 256:]], 2)

    def core_sums(products):
        sent = [fold(p[1]) for p in products]
        got = swap(jnp.stack(sent), "core")
        return [fold(p[0]) + got[n].astype(f32) for n, p in enumerate(products)]

    def row_parts(totals, index):
        taken = [lax.dynamic_index_in_dim(a, index, 0, keepdims=False) for a in totals]
        return jnp.stack(taken)

    def row_sends(totals):
        return [row_parts(totals, (row + d) % 4).astype(bf16) for d in (1, 2, 3)]

    def row_sums(totals, sends):
        result = row_parts(totals, row)
        for d in (1, 2, 3):
            result = result + shift(sends[d - 1], "row", d).astype(f32)
        return result

    def half_send(total):
        return lax.dynamic_index_in_dim(total, 1 - half, 1, keepdims=False).astype(bf16)

    def half_sum(total, sent):
        kept = lax.dynamic_index_in_dim(total, half, 1, keepdims=False)
        return kept + swap(sent, "half").astype(f32)

    outs = [narrow, wide, ((1, 1024), f32)]
    scratch = [((192, 1024), f32), ((192, 512), f32)]
    q3, g3, t3, sent, h = call(
        turn_kernel,
        [*outs, narrow, narrow],
        *got, *starts, top, x_rows[3], *weights[2],
        places=places, scratch=[*scratch, *values],
    )
    hidden.append(h)
    got = from_all(sent)
    products_a = [down_products(3, q3), up_products(3, top), up_products(2, g3)]
    got = after(got, [p[1] for p in products_a])
    q2, g2, t2, sent = call(
        backward_kernel,
        [*outs, narrow],
        *got, *saved[2], g3, x_rows[2], *weights[1],
        places=places, scratch=scratch,
    )
    got = from_all(sent)
    totals_a = core_sums(products_a)
    sends_a = row_sends(totals_a)
    products_b = [down_products(2, q2), up_products(1, g2)]
    got = after(got, sends_a + [p[1] for p in products_b])
    q1, g1, t1, sent = call(
        backward_kernel,
        [*outs, narrow],
        *got, *saved[1], g2, x_rows[1], *weights[0],
        places=places, scratch=scratch,
    )
    got = from_all(sent)
    totals_b = core_sums(products_b)
    sends_b = row_sends(totals_b)
    products_c = [down_products(1, q1), up_products(0, g1)]
    got = after(got, sends_b + [p[1] for p in products_c])
    q0, t0 = call(
        last_kernel,
        [narrow, ((1, 1024), f32)],
        *got, *saved[0], x_start, *weights[3],
        places=places, scratch=[((192, 512), f32)],
    )

    totals_c = core_sums(products_c)
    sends_c = row_sends(totals_c)
    rows_ab = jnp.concatenate([row_sums(totals_a, sends_a), row_sums(totals_b, sends_b)], 0)
    halves_ab = half_sum(rows_ab, half_send(rows_ab))

    gain_sums = jnp.concatenate([t0, t1, t2, t3], 0).reshape(16, 256)

    def with_gain(block, sums):
        high, low = two_parts(sums)
        return jnp.concatenate([block, high, low], 0)

    def gain_of(got):
        return got[:16].astype(f32) + got[16:].astype(f32)

    kept, sent = down_products(0, q0)
    got = swap(with_gain(sent, gain_sums), "core")
    total_d = (kept + got[:1024].astype(f32)).reshape(4, 2, 128, 256)
    gain_sums = gain_sums + gain_of(got[1024:])

    row_d = lax.dynamic_index_in_dim(total_d, row, 0, keepdims=False)
    gain_next = gain_sums
    for d in (1, 2, 3):
        part = lax.dynamic_index_in_dim(total_d, (row + d) % 4, 0, keepdims=False)
        got = shift(with_gain(part.reshape(256, 256).astype(bf16), gain_sums), "row", d)
        row_d = row_d + got[:256].astype(f32).reshape(2, 128, 256)
        gain_next = gain_next + gain_of(got[256:])
    rows_cd = jnp.concatenate([row_sums(totals_c, sends_c), row_d[None]], 0)
    got = swap(with_gain(half_send(rows_cd).reshape(384, 256), gain_next), "half")
    halves_cd = lax.dynamic_index_in_dim(rows_cd, half, 1, keepdims=False) + got[
        :384
    ].astype(f32).reshape(3, 128, 256)
    gain_sums = (gain_next + gain_of(got[384:])).reshape(4, 4, 256)

    down_3, up_3, up_2, down_2, up_1 = [halves_ab[n] for n in range(5)]
    down_1, up_0, down_0 = [halves_cd[n] for n in range(3)]
    sections = jnp.stack(
        [
            jnp.concatenate([a, b, gain_sums[s]], 0)
            for s, (a, b) in enumerate(
                ((down_0, up_0), (down_1, up_1), (down_2, up_2), (down_3, up_3))
            )
        ]
    )
    whole = lax.dynamic_index_in_dim(sections, seg, 0, keepdims=False)
    for d in (1, 2, 3):
        part = lax.dynamic_index_in_dim(sections, (seg + d) % 4, 0, keepdims=False)
        high, low = two_parts(part[256:])
        sent = jnp.concatenate([part[:256].astype(bf16), high, low, high, low], 0)
        got = shift(sent, "segment", d).astype(f32)
        whole = whole + jnp.concatenate([got[:256], got[256:260] + got[260:264]], 0)

    down_part = whole[:128]
    up_part = whole[128:256].reshape(2, 4, 2, 8, 256)
    up_mine = lax.dynamic_index_in_dim(up_part, core, 2, keepdims=False).reshape(64, 256)
    up_gone = lax.dynamic_index_in_dim(up_part, 1 - core, 2, keepdims=False).reshape(64, 256)
    kept = jnp.concatenate([pick(down_part, core, 64, 0), up_mine], 0)
    got = swap(jnp.concatenate([pick(down_part, 1 - core, 64, 0), up_gone], 0), "core")
    low = jnp.where(core == 0, kept, got)
    high = jnp.where(core == 0, got, kept)
    product = jnp.concatenate([low[:64], high[:64]], 1)
    quarters = [a.reshape(4, 8, 256) for a in (low[64:96], low[96:], high[64:96], high[96:])]
    up_rows = jnp.concatenate(quarters, 2)
    gain_rows = jnp.broadcast_to(whole[256:].reshape(1, 1, 1024), (4, 8, 1024))
    final = jnp.concatenate([up_rows, gain_rows], 1)

    final_blocks = [lax.dynamic_index_in_dim(final, col, 0, keepdims=False)]
    for t in (1, 2, 3):
        part = lax.dynamic_index_in_dim(final, (col + 4 - t) % 4, 0, keepdims=False)
        final_blocks.append(shift(part, "col", 4 - t))
    ordered = [choose(final_blocks, (t - col + 4) % 4) for t in range(4)]
    final = jnp.concatenate(
        [ordered[t][:, b * 128 : b * 128 + 128] for b in range(8) for t in range(4)], 1
    )
    up_out = final[:8]
    gain_out = final[8:9] / gain[None]
    place = ((row * 2 + half) * 4 + col) * 2 + core
    down_out = product * pick(gain, place, 64, 0)[:, None]
    return gain_out, down_out[None], up_out[None]


def solution(mesh):
    fine = Mesh(mesh.devices.reshape(4, 4, 2, 4, 2), ("segment",) + GROUPS)
    return jax.shard_map(
        per_device,
        mesh=fine,
        in_specs=(
            P(None, GROUPS, None),
            P(None, GROUPS, None),
            P("segment", None),
            P("segment", None, None),
            P("segment", None, None),
        ),
        out_specs=(P("segment", None), P("segment", GROUPS, None), P("segment", GROUPS, None)),
        check_vma=False,
    )
```

```python
import functools

import jax
import jax.numpy as jnp
from jax import lax
from jax.experimental import pallas as pl
from jax.experimental.pallas import tpu as pltpu
from jax.sharding import Mesh
from jax.sharding import PartitionSpec as P

eps = 1e-05
bf16 = jnp.bfloat16
f32 = jnp.float32
GROUPS = ("row", "half", "col", "core")
VMEM_BYTES = 12 * 1024 * 1024


def shift(block, axis, distance):
    count = lax.axis_size(axis)
    return lax.ppermute(block, axis, [(j, (j + distance) % count) for j in range(count)])


def swap(block, axis):
    return lax.ppermute(block, axis, [(0, 1), (1, 0)])


def dot(left, right, dims=((1,), (0,))):
    return lax.dot_general(left, right, (dims, ((), ())), preferred_element_type=f32)


def rows_product(left, right):
    return dot(left, right, ((0,), (0,)))


def gather4(block, axis):
    return [block] + [shift(block, axis, 4 - t) for t in (1, 2, 3)]


def from_all(block):
    return [block] + [shift(block, "col", d) for d in (1, 2, 3)]


def pick(array, index, size, axis):
    return lax.dynamic_slice_in_dim(array, index * size, size, axis=axis)


def choose(blocks, index):
    return lax.select_n(index.astype(jnp.int32), *blocks)


def after(arrays, first):
    return list(lax.optimization_barrier(tuple(arrays) + tuple(first)))[: len(arrays)]


def two_parts(array):
    high = lax.reduce_precision(array, 8, 7)
    return high.astype(bf16), (array - high).astype(bf16)


def call(kernel, outs, *operands, places, scratch=(), far_in=(), far_out=(), early=()):
    n_in, n_out = len(operands), len(outs)

    def body(place_ref, *refs):
        ins, results = list(refs[:n_in]), list(refs[n_in : n_in + n_out])
        more = list(refs[n_in + n_out :])
        extra = more[: len(scratch)]
        buffers = more[len(scratch) :]
        loads, stores = [], {}
        for n, k in enumerate(far_in):
            loads.append(pltpu.make_async_copy(ins[k], buffers[n], buffers[-1].at[n]))
            loads[-1].start()
            ins[k] = buffers[n]
        for n, k in enumerate(far_out):
            m = len(far_in) + n
            stores[k] = pltpu.make_async_copy(buffers[m], results[k], buffers[-1].at[m])
            results[k] = buffers[m]

        def settle():
            for copy in loads:
                copy.wait()
            for k in early:
                stores[k].start()

        kernel(settle, place_ref, *ins, *results, *extra)
        for k in far_out:
            if k not in early:
                stores[k].start()
        for k in far_out:
            stores[k].wait()

    near, far = pl.BlockSpec(memory_space=pltpu.VMEM), pl.BlockSpec(memory_space=pltpu.HBM)
    buffers = [pltpu.VMEM(shape, dtype) for shape, dtype in scratch]
    buffers += [pltpu.VMEM(operands[k].shape, operands[k].dtype) for k in far_in]
    buffers += [pltpu.VMEM(*outs[k]) for k in far_out]
    if far_in or far_out:
        buffers.append(pltpu.SemaphoreType.DMA((len(far_in) + len(far_out),)))
    return pl.pallas_call(
        body,
        out_shape=[jax.ShapeDtypeStruct(shape, dtype) for shape, dtype in outs],
        in_specs=[pl.BlockSpec(memory_space=pltpu.SMEM)]
        + [far if k in far_in else near for k in range(n_in)],
        out_specs=[far if k in far_out else near for k in range(n_out)],
        scratch_shapes=buffers,
        compiler_params=pltpu.CompilerParams(vmem_limit_bytes=VMEM_BYTES),
    )(places, *operands)


def silu_of(v):
    return (v / (1.0 + jnp.exp(-v))).astype(bf16)


def slope(v):
    logistic = 1.0 / (1.0 + jnp.exp(-v))
    return logistic * (1.0 + v * (1.0 - logistic))


def as_lanes(column):
    high = column.astype(bf16).astype(f32)
    lane = lax.broadcasted_iota(jnp.int32, (column.shape[0], 128), 1)
    return jnp.where(lane < 64, high, column - high).astype(bf16)


def of_lanes(block):
    return block[:, :1].astype(f32) + block[:, 64:65].astype(f32)


def prep_kernel(places, x_ref, top_ref, up_ref, p0, p1, p2, p3, piece, rms):
    col = places[1]
    for d, out in enumerate((p0, p1, p2, p3)):
        t = lax.rem(col + d, 4)
        for b in range(8):
            lanes = pl.ds(pl.multiple_of(b * 512 + t * 128, 128), 128)
            out[:48, b * 128 : b * 128 + 128] = x_ref[0, :, lanes]
            out[48:, b * 128 : b * 128 + 128] = top_ref[0, :, lanes]
    for b in range(8):
        lanes = pl.ds(pl.multiple_of(b * 512 + col * 128, 128), 128)
        low = (b // 4) * 128
        piece[low : low + 128, (b % 4) * 128 : (b % 4) * 128 + 128] = up_ref[:, lanes]
    squares = jnp.zeros((48, 1), f32)
    for b in range(4):
        wide = x_ref[0, :, b * 1024 : b * 1024 + 1024].astype(f32)
        squares = squares + jnp.sum(wide * wide, axis=-1, keepdims=True)
    rms[...] = as_lanes(lax.rsqrt(squares * (1.0 / 4096.0) + eps))


def prep(places, layer_inputs, top_cotangent, up):
    rows = pl.BlockSpec((1, 48, 4096), lambda g, p: (p[0], 0, 0))
    shapes = [(96, 1024)] * 4 + [(256, 512), (48, 128)]
    return pl.pallas_call(
        prep_kernel,
        grid_spec=pltpu.PrefetchScalarGridSpec(
            num_scalar_prefetch=1,
            grid=(1,),
            in_specs=[rows, rows, pl.BlockSpec((128, 4096), lambda g, p: (p[2], 0))],
            out_specs=[pl.BlockSpec(shape, lambda g, p: (0, 0)) for shape in shapes],
        ),
        out_shape=[jax.ShapeDtypeStruct(shape, bf16) for shape in shapes],
        compiler_params=pltpu.CompilerParams(vmem_limit_bytes=VMEM_BYTES),
    )(places, layer_inputs, top_cotangent, up)


def half_of(weights, part):
    return weights if part is None else weights.at[:, 256 * part : 256 * part + 256]


def grow(places, x_ref, h_ref, mine, other, x_out, sent):
    row, first = places[2], places[3] == 0
    grown = x_ref[...].astype(f32)
    for t in range(4):
        y = lax.rem(row + t, 4)
        h = h_ref[:, pl.ds(pl.multiple_of(y * 128, 128), 128)]
        part = jnp.where(first, mine[t], other[t])
        grown = grown + jnp.concatenate([dot(h, part[:128]), dot(h, part[128:])], 1)
    x_out[...] = grown.astype(bf16)
    wide = x_out[...].astype(f32)
    squares = jnp.sum(wide * wide, axis=-1, keepdims=True)
    total = jnp.zeros((192, 512), f32)
    for t in range(4):
        y = lax.rem(row + t, 4)
        rows = x_out[:, pl.ds(pl.multiple_of(y * 256, 128), 256)]
        total = total + dot(rows, jnp.where(first, other[t], mine[t]))
    sent[:, :512] = total.astype(bf16)
    sent[:, 512:] = as_lanes(squares)


def first_kernel(
    settle, places, b0, b1, b2, b3, x0, x1, x2, x3, mine, other,
    x_start, top, v, r, h, e, x_out, sent,
):
    for j, (b, x) in enumerate(zip((b0, b1, b2, b3), (x0, x1, x2, x3))):
        rows = slice(48 * j, 48 * j + 48)
        x_start[rows, :] = x[:48]
        top[rows, :] = x[48:]
        inverse_rms = of_lanes(b[:, 512:640])
        block = inverse_rms * b[:, :512].astype(f32)
        v[rows, :] = block
        r[rows, :] = jnp.broadcast_to(inverse_rms, (48, 128))
        h[rows, :] = silu_of(block)
        e[rows, :] = b[:, 640:]
    settle()
    grow(places, x_start, h, mine, other, x_out, sent)


def summed(refs, total, squares=None):
    own = refs[0]
    for j in range(4):
        rows = slice(48 * j, 48 * j + 48)
        value = own[rows, :512].astype(f32)
        if squares is not None:
            column = of_lanes(own[rows, 512:])
        for d in (1, 2, 3):
            low = 48 * ((j - d) % 4)
            value = value + refs[d][low : low + 48, :512].astype(f32)
            if squares is not None:
                column = column + of_lanes(refs[d][low : low + 48, 512:])
        total[rows, :] = value
        if squares is not None:
            squares[rows, :] = jnp.broadcast_to(column, (48, 128))


def normed(refs, v, r):
    summed(refs, v, r)
    r[...] = lax.rsqrt(r[...] * (1.0 / 4096.0) + eps)
    v[...] = r[:, :1] * v[...]


def forward_kernel(part, settle, places, p0, p1, p2, p3, x, mine, other, v, r, h, x_out, sent):
    normed((p0, p1, p2, p3), v, r)
    h[...] = silu_of(v[...])
    settle()
    grow(places, x, h, half_of(mine, part), half_of(other, part), x_out, sent)


def down_gradient(places, q_out, x, mine, other, acc, gain_sum):
    row, first = places[2], places[3] == 0
    for t in range(4):
        y = lax.rem(row + t, 4)
        lanes = pl.ds(pl.multiple_of(y * 256, 128), 256)
        added = dot(q_out[...], jnp.where(first, other[t], mine[t]), ((1,), (1,)))
        gain_sum[:, lanes] = jnp.sum(added * x[:, lanes].astype(f32), axis=0, keepdims=True)
        if acc is not None:
            acc[:, lanes] = acc[:, lanes] + added


def pass_back(places, e, v, r, g, x, mine, other, q_out, g_out, gain_sum, sent, acc):
    row, first = places[2], places[3] == 0
    contract = ((1,), (1,))
    inverse_rms = r[:, :1]
    value_grad = e[...].astype(f32) * slope(v[...]) * inverse_rms
    q_out[...] = value_grad.astype(bf16)
    pull = inverse_rms * (
        jnp.sum(value_grad * v[...], axis=-1, keepdims=True) * (1.0 / 4096.0)
    )
    acc[...] = g[...].astype(f32) - pull * x[...].astype(f32)
    down_gradient(places, q_out, x, mine, other, acc, gain_sum)
    g_out[...] = acc[...].astype(bf16)
    for t in range(4):
        y = lax.rem(row + t, 4)
        part = jnp.where(first, mine[t], other[t])
        product = dot(g_out[:, :512], part[:128], contract) + dot(
            g_out[:, 512:], part[128:], contract
        )
        sent[:, pl.ds(pl.multiple_of(y * 128, 128), 128)] = product.astype(bf16)


def turn_kernel(
    part, settle, places, p0, p1, p2, p3, e, g, x, mine, other,
    q_out, g_out, gain_sum, sent, h, acc, v, r,
):
    normed((p0, p1, p2, p3), v, r)
    h[...] = silu_of(v[...])
    settle()
    mine, other = half_of(mine, part), half_of(other, part)
    pass_back(places, e, v, r, g, x, mine, other, q_out, g_out, gain_sum, sent, acc)


def backward_kernel(
    part, settle, places, p0, p1, p2, p3, v, r, g, x, mine, other,
    q_out, g_out, gain_sum, sent, acc, e,
):
    summed((p0, p1, p2, p3), e)
    settle()
    mine, other = half_of(mine, part), half_of(other, part)
    pass_back(places, e, v, r, g, x, mine, other, q_out, g_out, gain_sum, sent, acc)


def last_kernel(settle, places, p0, p1, p2, p3, v, r, x, mine, other, q_out, gain_sum, e):
    summed((p0, p1, p2, p3), e)
    settle()
    q_out[...] = (e[...] * slope(v[...]) * r[:, :1]).astype(bf16)
    down_gradient(places, q_out, x, mine, other, None, gain_sum)


def per_device(layer_inputs, top_cotangent, norm_gains, down_weight, up_weight):
    seg = lax.axis_index("segment")
    row = lax.axis_index("row")
    half = lax.axis_index("half")
    col = lax.axis_index("col")
    core = lax.axis_index("core")
    places = jnp.stack([seg, col, row, core]).astype(jnp.int32)
    gain = norm_gains[0]
    down = down_weight[0]
    up = up_weight[0]

    *parts, up_piece, start_rms = prep(places, layer_inputs, top_cotangent, up)

    down_piece = jnp.concatenate(
        [
            lax.dynamic_slice_in_dim(down, ((row * 2 + b) * 4 + col) * 128, 128, axis=0).astype(f32)
            * lax.dynamic_slice_in_dim(gain, ((row * 2 + b) * 4 + col) * 128, 128, axis=0)[:, None]
            for b in (0, 1)
        ],
        0,
    ).astype(bf16)
    scaled = (layer_inputs.astype(f32) * gain).astype(bf16).reshape(192, 4096)
    first = dot(scaled, down).reshape(4, 48, 512).astype(bf16)
    last = dot(top_cotangent.reshape(192, 4096), up, ((1,), (1,))).reshape(4, 48, 512).astype(bf16)
    piece = jnp.where(core == 0, up_piece, down_piece)
    x_blocks = [parts[0]] + [shift(parts[d], "col", d) for d in (1, 2, 3)]
    passed = [first[0]]
    pieces = [piece]
    for d in (1, 2, 3):
        rows = jnp.where(seg == 0, first[d], last[d - 1])
        got = shift(jnp.concatenate([piece, rows], 0), "segment", d)
        passed.append(got[256:])
        pieces.append(got[:256])
    passed.append(last[3])
    pieces = [pieces[0], pieces[3], pieces[2], pieces[1]]
    pieces = after(pieces, x_blocks[1:])
    start = jnp.concatenate(
        [choose(passed[:4], seg), start_rms, choose(passed[1:], seg)], 1
    )
    starts = from_all(start)

    def own_piece(s):
        return choose(pieces, (s + core - seg + 4) % 4)

    blocks = [gather4(own_piece(0), "row")]
    pair = jnp.concatenate([own_piece(1), own_piece(2)], 0)
    blocks.append(gather4(after([pair], blocks[0][1:])[0], "row"))

    wide, narrow = ((192, 1024), bf16), ((192, 512), bf16)
    values = [((192, 512), f32), ((192, 128), f32)]
    mine = jnp.stack(after(blocks[0], starts))
    weights = [(mine, swap(mine, "core"))]
    x_start, top, v, r, h, last_e, x_next, sent = call(
        first_kernel,
        [wide, wide, *values, narrow, narrow, wide, ((192, 640), bf16)],
        *starts, *x_blocks, *weights[0],
        places=places, far_out=range(7), early=range(6),
    )
    x_rows, hidden, saved = [x_start, x_next], [h], [(v, r)]
    for s in (1, 2):
        got = from_all(sent)
        if s == 1:
            mine = jnp.stack(after(blocks[1], got[1:]))
            weights += [(mine, swap(mine, "core"))] * 2
        else:
            (own,) = after([own_piece(3)], got[1:])
            near = [shift(own, "row", 3), shift(own, "row", 1)]
        v, r, h, x_next, sent = call(
            functools.partial(forward_kernel, s - 1),
            [*values, narrow, wide, ((192, 640), bf16)],
            *got, x_rows[s], *weights[s],
            places=places, far_in=(4,), far_out=range(4), early=range(3),
        )
        x_rows.append(x_next)
        hidden.append(h)
        saved.append((v, r))
    got = from_all(sent)
    (own,) = after([own], got[1:] + near)
    far = shift(own, "row", 2)
    got = after(got, [own])

    def down_products(s, q):
        kept = rows_product(x_rows[s], pick(q, core, 256, 1))
        return kept, rows_product(x_rows[s], pick(q, 1 - core, 256, 1)).astype(bf16)

    def up_products(s, g):
        kept = rows_product(hidden[s], pick(g, core, 512, 1))
        return kept, rows_product(hidden[s], pick(g, 1 - core, 512, 1)).astype(bf16)

    def fold(product):
        if product.shape[1] == 256:
            return product.reshape(4, 2, 128, 256)
        lanes = product.reshape(4, 2, 64, 512)
        return jnp.concatenate([lanes[..., :256], lanes[..., 256:]], 2)

    def core_swap(products):
        return swap(jnp.stack([fold(p[1]) for p in products]), "core")

    def core_sums(products, got):
        return jnp.stack([fold(p[0]) for p in products]) + got.astype(f32)

    def at(array, index, axis):
        return lax.dynamic_index_in_dim(array, index, axis, keepdims=False)

    def row_sends(totals):
        return [at(totals, (row + d) % 4, 1).astype(bf16) for d in (1, 2, 3)]

    def row_sums(totals, sends):
        result = at(totals, row, 1)
        for d in (1, 2, 3):
            result = result + shift(sends[d - 1], "row", d).astype(f32)
        return result

    outs = [narrow, wide, ((1, 1024), f32)]
    scratch = [((192, 1024), f32), ((192, 512), f32)]
    q3, g3, t3, sent, h = call(
        functools.partial(turn_kernel, 1),
        [*outs, narrow, narrow],
        *got, last_e, top, x_rows[3], *weights[2],
        places=places, scratch=[scratch[0], *values], far_in=(4, 5, 6),
    )
    hidden.append(h)
    got = from_all(sent)
    products_a = [down_products(3, q3), up_products(3, top), up_products(2, g3)]
    mine = jnp.stack(after([own, near[0], far, near[1]], got[1:]))
    weights.append((mine, swap(mine, "core")))
    totals_a = core_sums(products_a, *after([core_swap(products_a)], got[1:]))
    half_a = at(totals_a, 1 - half, 2).astype(bf16)
    got = after(got, [half_a])
    q2, g2, t2, sent = call(
        functools.partial(backward_kernel, 0),
        [*outs, narrow],
        *got, *saved[2], g3, x_rows[2], *weights[1],
        places=places, scratch=scratch, far_in=(4, 5, 7),
    )
    got = from_all(sent)
    products_b = [down_products(2, q2), up_products(1, g2)]
    totals_b = core_sums(products_b, *after([core_swap(products_b)], got[1:]))
    half_b = at(totals_b, 1 - half, 2).astype(bf16)
    got = after(got, [half_b])
    q1, g1, t1, sent = call(
        functools.partial(backward_kernel, None),
        [*outs, narrow],
        *got, *saved[1], g2, x_rows[1], *weights[0],
        places=places, scratch=scratch, far_in=(4, 5, 7),
    )
    got = from_all(sent)
    products_c = [down_products(1, q1), up_products(0, g1)]
    from_a, from_b, from_core = after(
        [swap(half_a, "half"), swap(half_b, "half"), core_swap(products_c)], got[1:]
    )
    totals_ab = jnp.concatenate(
        [
            at(totals_a, half, 2) + from_a.astype(f32),
            at(totals_b, half, 2) + from_b.astype(f32),
        ],
        0,
    )
    sends_ab = row_sends(totals_ab)
    totals_c = core_sums(products_c, from_core)
    half_c = at(totals_c, 1 - half, 2).astype(bf16)
    got = after(got, [*sends_ab, half_c])
    q0, t0 = call(
        last_kernel,
        [narrow, ((1, 1024), f32)],
        *got, *saved[0], x_start, *weights[3],
        places=places, scratch=[((192, 512), f32)], far_in=(4, 5, 6),
    )

    sums_ab = row_sums(totals_ab, sends_ab)
    totals_c = at(totals_c, half, 2) + swap(half_c, "half").astype(f32)

    gain_sums = jnp.concatenate([t0, t1, t2, t3], 0).reshape(16, 256)

    def with_gain(block, sums):
        high, low = two_parts(sums)
        return jnp.concatenate([block, high, low], 0)

    def gain_of(got):
        return got[:16].astype(f32) + got[16:].astype(f32)

    kept, sent = down_products(0, q0)
    got = swap(with_gain(sent, gain_sums), "core")
    total_d = (kept + got[:1024].astype(f32)).reshape(4, 2, 128, 256)
    gain_sums = gain_sums + gain_of(got[1024:])

    def row_cd(index):
        part = [at(totals_c, index, 1).reshape(256, 256), at(total_d, index, 0).reshape(256, 256)]
        return jnp.concatenate(part, 0)

    sums_cd, gain_next = row_cd(row), gain_sums
    for d in (1, 2, 3):
        sent = with_gain(row_cd((row + d) % 4).astype(bf16), gain_sums)
        got = shift(sent, "row", d)
        sums_cd = sums_cd + got[:512].astype(f32)
        gain_next = gain_next + gain_of(got[512:])
    row_d = sums_cd[256:].reshape(2, 128, 256)
    got = swap(with_gain(at(row_d, 1 - half, 0).astype(bf16), gain_next), "half")
    down_0 = at(row_d, half, 0) + got[:128].astype(f32)
    gain_next = gain_next + gain_of(got[128:])
    gain_sums = gain_next.reshape(4, 4, 256)

    down_3, up_3, up_2, down_2, up_1 = [sums_ab[n] for n in range(5)]
    down_1, up_0 = sums_cd[:128], sums_cd[128:256]
    sections = jnp.stack(
        [
            jnp.concatenate([a, b, gain_sums[s]], 0)
            for s, (a, b) in enumerate(
                ((down_0, up_0), (down_1, up_1), (down_2, up_2), (down_3, up_3))
            )
        ]
    )
    whole = lax.dynamic_index_in_dim(sections, seg, 0, keepdims=False)
    for d in (1, 2, 3):
        part = lax.dynamic_index_in_dim(sections, (seg + d) % 4, 0, keepdims=False)
        high, low = two_parts(part[256:])
        sent = jnp.concatenate([part[:256].astype(bf16), high, low, high, low], 0)
        got = shift(sent, "segment", d).astype(f32)
        whole = whole + jnp.concatenate([got[:256], got[256:260] + got[260:264]], 0)

    down_part = whole[:128]
    up_part = whole[128:256].reshape(2, 4, 2, 8, 256)
    up_mine = lax.dynamic_index_in_dim(up_part, core, 2, keepdims=False).reshape(64, 256)
    up_gone = lax.dynamic_index_in_dim(up_part, 1 - core, 2, keepdims=False).reshape(64, 256)
    kept = jnp.concatenate([pick(down_part, core, 64, 0), up_mine], 0)
    got = swap(jnp.concatenate([pick(down_part, 1 - core, 64, 0), up_gone], 0), "core")
    low = jnp.where(core == 0, kept, got)
    high = jnp.where(core == 0, got, kept)
    product = jnp.concatenate([low[:64], high[:64]], 1)
    quarters = [a.reshape(4, 8, 256) for a in (low[64:96], low[96:], high[64:96], high[96:])]
    up_rows = jnp.concatenate(quarters, 2)
    gain_rows = jnp.broadcast_to(whole[256:].reshape(1, 1, 1024), (4, 8, 1024))
    final = jnp.concatenate([up_rows, gain_rows], 1)

    final_blocks = [lax.dynamic_index_in_dim(final, col, 0, keepdims=False)]
    for t in (1, 2, 3):
        part = lax.dynamic_index_in_dim(final, (col + 4 - t) % 4, 0, keepdims=False)
        final_blocks.append(shift(part, "col", 4 - t))
    ordered = [choose(final_blocks, (t - col + 4) % 4) for t in range(4)]
    final = jnp.concatenate(
        [ordered[t][:, b * 128 : b * 128 + 128] for b in range(8) for t in range(4)], 1
    )
    up_out = final[:8]
    gain_out = final[8:9] / gain[None]
    place = ((row * 2 + half) * 4 + col) * 2 + core
    down_out = product * pick(gain, place, 64, 0)[:, None]
    return gain_out, down_out[None], up_out[None]


def solution(mesh):
    fine = Mesh(mesh.devices.reshape(4, 4, 2, 4, 2), ("segment",) + GROUPS)
    return jax.shard_map(
        per_device,
        mesh=fine,
        in_specs=(
            P(None, GROUPS, None),
            P(None, GROUPS, None),
            P("segment", None),
            P("segment", None, None),
            P("segment", None, None),
        ),
        out_specs=(P("segment", None), P("segment", GROUPS, None), P("segment", GROUPS, None)),
        check_vma=False,
    )
```

```python
import functools

import jax
import jax.numpy as jnp
from jax import lax
from jax.experimental import pallas as pl
from jax.experimental.pallas import tpu as pltpu
from jax.sharding import Mesh
from jax.sharding import PartitionSpec as P

eps = 1e-05
bf16 = jnp.bfloat16
f32 = jnp.float32
GROUPS = ("row", "half", "col", "core")
VMEM_BYTES = 8 * 1024 * 1024


def shift(block, axis, distance):
    count = lax.axis_size(axis)
    return lax.ppermute(block, axis, [(j, (j + distance) % count) for j in range(count)])


def swap(block, axis):
    return lax.ppermute(block, axis, [(0, 1), (1, 0)])


def dot(left, right, dims=((1,), (0,))):
    return lax.dot_general(left, right, (dims, ((), ())), preferred_element_type=f32)


def rows_product(left, right):
    return dot(left, right, ((0,), (0,)))


def gather4(block, axis):
    return [block] + [shift(block, axis, 4 - t) for t in (1, 2, 3)]


def from_all(block):
    return [block] + [shift(block, "col", d) for d in (1, 2, 3)]


def pick(array, index, size, axis):
    return lax.dynamic_slice_in_dim(array, index * size, size, axis=axis)


def choose(blocks, index):
    return lax.select_n(index.astype(jnp.int32), *blocks)


def after(arrays, first):
    return list(lax.optimization_barrier(tuple(arrays) + tuple(first)))[: len(arrays)]


def two_parts(array):
    high = lax.reduce_precision(array, 8, 7)
    return high.astype(bf16), (array - high).astype(bf16)


def call(kernel, outs, *operands, places, scratch=()):
    whole = pl.BlockSpec(memory_space=pltpu.VMEM)
    return pl.pallas_call(
        kernel,
        out_shape=[jax.ShapeDtypeStruct(shape, dtype) for shape, dtype in outs],
        in_specs=[pl.BlockSpec(memory_space=pltpu.SMEM)] + [whole] * len(operands),
        out_specs=[whole] * len(outs),
        scratch_shapes=[pltpu.VMEM(shape, dtype) for shape, dtype in scratch],
        compiler_params=pltpu.CompilerParams(vmem_limit_bytes=VMEM_BYTES),
    )(places, *operands)


def silu_of(v):
    return (v / (1.0 + jnp.exp(-v))).astype(bf16)


def slope(v):
    logistic = 1.0 / (1.0 + jnp.exp(-v))
    return logistic * (1.0 + v * (1.0 - logistic))


def as_lanes(column):
    high = column.astype(bf16).astype(f32)
    lane = lax.broadcasted_iota(jnp.int32, (column.shape[0], 128), 1)
    return jnp.where(lane < 64, high, column - high).astype(bf16)


def of_lanes(block):
    return block[:, :1].astype(f32) + block[:, 64:65].astype(f32)


def prep_kernel(places, x_ref, top_ref, up_ref, p0, p1, p2, p3, piece, rms):
    col = places[1]
    for d, out in enumerate((p0, p1, p2, p3)):
        t = lax.rem(col + d, 4)
        for b in range(8):
            lanes = pl.ds(pl.multiple_of(b * 512 + t * 128, 128), 128)
            out[:48, b * 128 : b * 128 + 128] = x_ref[0, :, lanes]
            out[48:, b * 128 : b * 128 + 128] = top_ref[0, :, lanes]
    for b in range(8):
        lanes = pl.ds(pl.multiple_of(b * 512 + col * 128, 128), 128)
        low = (b // 4) * 128
        piece[low : low + 128, (b % 4) * 128 : (b % 4) * 128 + 128] = up_ref[:, lanes]
    squares = jnp.zeros((48, 1), f32)
    for b in range(4):
        wide = x_ref[0, :, b * 1024 : b * 1024 + 1024].astype(f32)
        squares = squares + jnp.sum(wide * wide, axis=-1, keepdims=True)
    rms[...] = as_lanes(lax.rsqrt(squares * (1.0 / 4096.0) + eps))


def prep(places, layer_inputs, top_cotangent, up):
    rows = pl.BlockSpec((1, 48, 4096), lambda g, p: (p[0], 0, 0))
    shapes = [(96, 1024)] * 4 + [(256, 512), (48, 128)]
    return pl.pallas_call(
        prep_kernel,
        grid_spec=pltpu.PrefetchScalarGridSpec(
            num_scalar_prefetch=1,
            grid=(1,),
            in_specs=[rows, rows, pl.BlockSpec((128, 4096), lambda g, p: (p[2], 0))],
            out_specs=[pl.BlockSpec(shape, lambda g, p: (0, 0)) for shape in shapes],
        ),
        out_shape=[jax.ShapeDtypeStruct(shape, bf16) for shape in shapes],
        compiler_params=pltpu.CompilerParams(vmem_limit_bytes=VMEM_BYTES),
    )(places, layer_inputs, top_cotangent, up)


def half_of(weights, part):
    return weights if part is None else weights.at[:, 256 * part : 256 * part + 256]


def grow(places, x_ref, h_ref, mine, other, x_out, sent):
    row, first = places[2], places[3] == 0
    grown = x_ref[...].astype(f32)
    for t in range(4):
        y = lax.rem(row + t, 4)
        h = h_ref[:, pl.ds(pl.multiple_of(y * 128, 128), 128)]
        part = jnp.where(first, mine[t], other[t])
        grown = grown + jnp.concatenate([dot(h, part[:128]), dot(h, part[128:])], 1)
    x_out[...] = grown.astype(bf16)
    wide = x_out[...].astype(f32)
    squares = jnp.sum(wide * wide, axis=-1, keepdims=True)
    total = jnp.zeros((192, 512), f32)
    for t in range(4):
        y = lax.rem(row + t, 4)
        rows = x_out[:, pl.ds(pl.multiple_of(y * 256, 128), 256)]
        total = total + dot(rows, jnp.where(first, other[t], mine[t]))
    sent[:, :512] = total.astype(bf16)
    sent[:, 512:] = as_lanes(squares)


def first_kernel(
    places, b0, b1, b2, b3, x0, x1, x2, x3, mine, other,
    x_start, top, v, r, h, e, x_out, sent,
):
    for j, (b, x) in enumerate(zip((b0, b1, b2, b3), (x0, x1, x2, x3))):
        rows = slice(48 * j, 48 * j + 48)
        x_start[rows, :] = x[:48]
        top[rows, :] = x[48:]
        inverse_rms = of_lanes(b[:, 512:640])
        block = inverse_rms * b[:, :512].astype(f32)
        v[rows, :] = block
        r[rows, :] = jnp.broadcast_to(inverse_rms, (48, 128))
        h[rows, :] = silu_of(block)
        e[rows, :] = b[:, 640:]
    grow(places, x_start, h, mine, other, x_out, sent)


def summed(refs, total, squares=None):
    own = refs[0]
    for j in range(4):
        rows = slice(48 * j, 48 * j + 48)
        value = own[rows, :512].astype(f32)
        if squares is not None:
            column = of_lanes(own[rows, 512:])
        for d in (1, 2, 3):
            low = 48 * ((j - d) % 4)
            value = value + refs[d][low : low + 48, :512].astype(f32)
            if squares is not None:
                column = column + of_lanes(refs[d][low : low + 48, 512:])
        total[rows, :] = value
        if squares is not None:
            squares[rows, :] = jnp.broadcast_to(column, (48, 128))


def normed(refs, v, r):
    summed(refs, v, r)
    r[...] = lax.rsqrt(r[...] * (1.0 / 4096.0) + eps)
    v[...] = r[:, :1] * v[...]


def forward_kernel(part, places, p0, p1, p2, p3, x, mine, other, v, r, h, x_out, sent):
    normed((p0, p1, p2, p3), v, r)
    h[...] = silu_of(v[...])
    grow(places, x, h, half_of(mine, part), half_of(other, part), x_out, sent)


def down_gradient(places, q_out, x, mine, other, acc, gain_sum):
    row, first = places[2], places[3] == 0
    for t in range(4):
        y = lax.rem(row + t, 4)
        lanes = pl.ds(pl.multiple_of(y * 256, 128), 256)
        added = dot(q_out[...], jnp.where(first, other[t], mine[t]), ((1,), (1,)))
        gain_sum[:, lanes] = jnp.sum(added * x[:, lanes].astype(f32), axis=0, keepdims=True)
        if acc is not None:
            acc[:, lanes] = acc[:, lanes] + added


def pass_back(places, e, v, r, g, x, mine, other, q_out, g_out, gain_sum, sent, acc):
    row, first = places[2], places[3] == 0
    contract = ((1,), (1,))
    inverse_rms = r[:, :1]
    value_grad = e[...].astype(f32) * slope(v[...]) * inverse_rms
    q_out[...] = value_grad.astype(bf16)
    pull = inverse_rms * (
        jnp.sum(value_grad * v[...], axis=-1, keepdims=True) * (1.0 / 4096.0)
    )
    acc[...] = g[...].astype(f32) - pull * x[...].astype(f32)
    down_gradient(places, q_out, x, mine, other, acc, gain_sum)
    g_out[...] = acc[...].astype(bf16)
    for t in range(4):
        y = lax.rem(row + t, 4)
        part = jnp.where(first, mine[t], other[t])
        product = dot(g_out[:, :512], part[:128], contract) + dot(
            g_out[:, 512:], part[128:], contract
        )
        sent[:, pl.ds(pl.multiple_of(y * 128, 128), 128)] = product.astype(bf16)


def turn_kernel(
    part, places, p0, p1, p2, p3, e, g, x, mine, other,
    q_out, g_out, gain_sum, sent, h, acc, v, r,
):
    normed((p0, p1, p2, p3), v, r)
    h[...] = silu_of(v[...])
    mine, other = half_of(mine, part), half_of(other, part)
    pass_back(places, e, v, r, g, x, mine, other, q_out, g_out, gain_sum, sent, acc)


def backward_kernel(
    part, places, p0, p1, p2, p3, v, r, g, x, mine, other,
    q_out, g_out, gain_sum, sent, acc, e,
):
    summed((p0, p1, p2, p3), e)
    mine, other = half_of(mine, part), half_of(other, part)
    pass_back(places, e, v, r, g, x, mine, other, q_out, g_out, gain_sum, sent, acc)


def last_kernel(places, p0, p1, p2, p3, v, r, x, mine, other, q_out, gain_sum, e):
    summed((p0, p1, p2, p3), e)
    q_out[...] = (e[...] * slope(v[...]) * r[:, :1]).astype(bf16)
    down_gradient(places, q_out, x, mine, other, None, gain_sum)


def per_device(layer_inputs, top_cotangent, norm_gains, down_weight, up_weight):
    seg = lax.axis_index("segment")
    row = lax.axis_index("row")
    half = lax.axis_index("half")
    col = lax.axis_index("col")
    core = lax.axis_index("core")
    places = jnp.stack([seg, col, row, core]).astype(jnp.int32)
    gain = norm_gains[0]
    down = down_weight[0]
    up = up_weight[0]

    *parts, up_piece, start_rms = prep(places, layer_inputs, top_cotangent, up)

    down_piece = jnp.concatenate(
        [
            lax.dynamic_slice_in_dim(down, ((row * 2 + b) * 4 + col) * 128, 128, axis=0).astype(f32)
            * lax.dynamic_slice_in_dim(gain, ((row * 2 + b) * 4 + col) * 128, 128, axis=0)[:, None]
            for b in (0, 1)
        ],
        0,
    ).astype(bf16)
    scaled = (layer_inputs.astype(f32) * gain).astype(bf16).reshape(192, 4096)
    first = dot(scaled, down).reshape(4, 48, 512).astype(bf16)
    last = dot(top_cotangent.reshape(192, 4096), up, ((1,), (1,))).reshape(4, 48, 512).astype(bf16)
    piece = jnp.where(core == 0, up_piece, down_piece)
    x_blocks = [parts[0]] + [shift(parts[d], "col", d) for d in (1, 2, 3)]
    passed = [first[0]]
    pieces = [piece]
    for d in (1, 2, 3):
        rows = jnp.where(seg == 0, first[d], last[d - 1])
        got = shift(jnp.concatenate([piece, rows], 0), "segment", d)
        passed.append(got[256:])
        pieces.append(got[:256])
    passed.append(last[3])
    pieces = [pieces[0], pieces[3], pieces[2], pieces[1]]
    pieces = after(pieces, x_blocks[1:])
    start = jnp.concatenate(
        [choose(passed[:4], seg), start_rms, choose(passed[1:], seg)], 1
    )
    starts = from_all(start)

    def own_piece(s):
        return choose(pieces, (s + core - seg + 4) % 4)

    blocks = [gather4(own_piece(0), "row")]
    pair = jnp.concatenate([own_piece(1), own_piece(2)], 0)
    blocks.append(gather4(after([pair], blocks[0][1:])[0], "row"))

    wide, narrow = ((192, 1024), bf16), ((192, 512), bf16)
    values = [((192, 512), f32), ((192, 128), f32)]
    mine = jnp.stack(after(blocks[0], starts))
    weights = [(mine, swap(mine, "core"))]
    x_start, top, v, r, h, last_e, x_next, sent = call(
        first_kernel,
        [wide, wide, *values, narrow, narrow, wide, ((192, 640), bf16)],
        *starts, *x_blocks, *weights[0],
        places=places,
    )
    x_rows, hidden, saved = [x_start, x_next], [h], [(v, r)]
    for s in (1, 2):
        got = from_all(sent)
        if s == 1:
            mine = jnp.stack(after(blocks[1], got[1:]))
            weights += [(mine, swap(mine, "core"))] * 2
        else:
            (own,) = after([own_piece(3)], got[1:])
            near = [shift(own, "row", 3), shift(own, "row", 1)]
        v, r, h, x_next, sent = call(
            functools.partial(forward_kernel, s - 1),
            [*values, narrow, wide, ((192, 640), bf16)],
            *got, x_rows[s], *weights[s],
            places=places,
        )
        x_rows.append(x_next)
        hidden.append(h)
        saved.append((v, r))
    got = from_all(sent)
    (own,) = after([own], got[1:] + near)
    far = shift(own, "row", 2)
    got = after(got, [own])

    def down_products(s, q):
        kept = rows_product(x_rows[s], pick(q, core, 256, 1))
        return kept, rows_product(x_rows[s], pick(q, 1 - core, 256, 1)).astype(bf16)

    def up_products(s, g):
        kept = rows_product(hidden[s], pick(g, core, 512, 1))
        return kept, rows_product(hidden[s], pick(g, 1 - core, 512, 1)).astype(bf16)

    def fold(product):
        if product.shape[1] == 256:
            return product.reshape(4, 2, 128, 256)
        lanes = product.reshape(4, 2, 64, 512)
        return jnp.concatenate([lanes[..., :256], lanes[..., 256:]], 2)

    def core_swap(products):
        return swap(jnp.stack([fold(p[1]) for p in products]), "core")

    def core_sums(products, got):
        return jnp.stack([fold(p[0]) for p in products]) + got.astype(f32)

    def at(array, index, axis):
        return lax.dynamic_index_in_dim(array, index, axis, keepdims=False)

    def row_sends(totals):
        return [at(totals, (row + d) % 4, 1).astype(bf16) for d in (1, 2, 3)]

    def row_sums(totals, sends):
        result = at(totals, row, 1)
        for d in (1, 2, 3):
            result = result + shift(sends[d - 1], "row", d).astype(f32)
        return result

    outs = [narrow, wide, ((1, 1024), f32)]
    scratch = [((192, 1024), f32), ((192, 512), f32)]
    q3, g3, t3, sent, h = call(
        functools.partial(turn_kernel, 1),
        [*outs, narrow, narrow],
        *got, last_e, top, x_rows[3], *weights[2],
        places=places, scratch=[scratch[0], *values],
    )
    hidden.append(h)
    got = from_all(sent)
    products_a = [down_products(3, q3), up_products(3, top), up_products(2, g3)]
    mine = jnp.stack(after([own, near[0], far, near[1]], got[1:]))
    weights.append((mine, swap(mine, "core")))
    totals_a = core_sums(products_a, *after([core_swap(products_a)], got[1:]))
    half_a = at(totals_a, 1 - half, 2).astype(bf16)
    got = after(got, [half_a])
    q2, g2, t2, sent = call(
        functools.partial(backward_kernel, 0),
        [*outs, narrow],
        *got, *saved[2], g3, x_rows[2], *weights[1],
        places=places, scratch=scratch,
    )
    got = from_all(sent)
    products_b = [down_products(2, q2), up_products(1, g2)]
    totals_b = core_sums(products_b, *after([core_swap(products_b)], got[1:]))
    half_b = at(totals_b, 1 - half, 2).astype(bf16)
    got = after(got, [half_b])
    q1, g1, t1, sent = call(
        functools.partial(backward_kernel, None),
        [*outs, narrow],
        *got, *saved[1], g2, x_rows[1], *weights[0],
        places=places, scratch=scratch,
    )
    got = from_all(sent)
    products_c = [down_products(1, q1), up_products(0, g1)]
    from_a, from_b, from_core = after(
        [swap(half_a, "half"), swap(half_b, "half"), core_swap(products_c)], got[1:]
    )
    totals_ab = jnp.concatenate(
        [
            at(totals_a, half, 2) + from_a.astype(f32),
            at(totals_b, half, 2) + from_b.astype(f32),
        ],
        0,
    )
    sends_ab = row_sends(totals_ab)
    totals_c = core_sums(products_c, from_core)
    half_c = at(totals_c, 1 - half, 2).astype(bf16)
    got = after(got, [*sends_ab, half_c])
    q0, t0 = call(
        last_kernel,
        [narrow, ((1, 1024), f32)],
        *got, *saved[0], x_start, *weights[3],
        places=places, scratch=[((192, 512), f32)],
    )

    sums_ab = row_sums(totals_ab, sends_ab)
    totals_c = at(totals_c, half, 2) + swap(half_c, "half").astype(f32)

    gain_sums = jnp.concatenate([t0, t1, t2, t3], 0).reshape(16, 256)

    def with_gain(block, sums):
        high, low = two_parts(sums)
        return jnp.concatenate([block, high, low], 0)

    def gain_of(got):
        return got[:16].astype(f32) + got[16:].astype(f32)

    kept, sent = down_products(0, q0)
    got = swap(with_gain(sent, gain_sums), "core")
    total_d = (kept + got[:1024].astype(f32)).reshape(4, 2, 128, 256)
    gain_sums = gain_sums + gain_of(got[1024:])

    half_d = at(total_d, 1 - half, 1).astype(bf16).reshape(512, 256)
    got = swap(with_gain(half_d, gain_sums), "half")
    total_d = at(total_d, half, 1) + got[:512].astype(f32).reshape(4, 128, 256)
    gain_sums = gain_sums + gain_of(got[512:])
    totals_cd = jnp.concatenate([totals_c, total_d[None]], 0)

    def row_cd(index):
        return at(totals_cd, index, 1).reshape(384, 256)

    sums_cd, gain_next = row_cd(row), gain_sums
    for d in (1, 2, 3):
        sent = with_gain(row_cd((row + d) % 4).astype(bf16), gain_sums)
        got = shift(sent, "row", d)
        sums_cd = sums_cd + got[:384].astype(f32)
        gain_next = gain_next + gain_of(got[384:])
    down_0 = sums_cd[256:]
    gain_sums = gain_next.reshape(4, 4, 256)

    down_3, up_3, up_2, down_2, up_1 = [sums_ab[n] for n in range(5)]
    down_1, up_0 = sums_cd[:128], sums_cd[128:256]
    sections = jnp.stack(
        [
            jnp.concatenate([a, b, gain_sums[s]], 0)
            for s, (a, b) in enumerate(
                ((down_0, up_0), (down_1, up_1), (down_2, up_2), (down_3, up_3))
            )
        ]
    )
    whole = lax.dynamic_index_in_dim(sections, seg, 0, keepdims=False)
    for d in (1, 2, 3):
        part = lax.dynamic_index_in_dim(sections, (seg + d) % 4, 0, keepdims=False)
        high, low = two_parts(part[256:])
        sent = jnp.concatenate([part[:256].astype(bf16), high, low, high, low], 0)
        got = shift(sent, "segment", d).astype(f32)
        whole = whole + jnp.concatenate([got[:256], got[256:260] + got[260:264]], 0)

    down_part = whole[:128]
    up_part = whole[128:256].reshape(2, 4, 2, 8, 256)
    up_mine = lax.dynamic_index_in_dim(up_part, core, 2, keepdims=False).reshape(64, 256)
    up_gone = lax.dynamic_index_in_dim(up_part, 1 - core, 2, keepdims=False).reshape(64, 256)
    kept = jnp.concatenate([pick(down_part, core, 64, 0), up_mine], 0)
    got = swap(jnp.concatenate([pick(down_part, 1 - core, 64, 0), up_gone], 0), "core")
    low = jnp.where(core == 0, kept, got)
    high = jnp.where(core == 0, got, kept)
    product = jnp.concatenate([low[:64], high[:64]], 1)
    quarters = [a.reshape(4, 8, 256) for a in (low[64:96], low[96:], high[64:96], high[96:])]
    up_rows = jnp.concatenate(quarters, 2)
    gain_rows = jnp.broadcast_to(whole[256:].reshape(1, 1, 1024), (4, 8, 1024))
    final = jnp.concatenate([up_rows, gain_rows], 1)

    final_blocks = [lax.dynamic_index_in_dim(final, col, 0, keepdims=False)]
    for t in (1, 2, 3):
        part = lax.dynamic_index_in_dim(final, (col + 4 - t) % 4, 0, keepdims=False)
        final_blocks.append(shift(part, "col", 4 - t))
    ordered = [choose(final_blocks, (t - col + 4) % 4) for t in range(4)]
    final = jnp.concatenate(
        [ordered[t][:, b * 128 : b * 128 + 128] for b in range(8) for t in range(4)], 1
    )
    up_out = final[:8]
    gain_out = final[8:9] / gain[None]
    place = ((row * 2 + half) * 4 + col) * 2 + core
    down_out = product * pick(gain, place, 64, 0)[:, None]
    return gain_out, down_out[None], up_out[None]


def solution(mesh):
    fine = Mesh(mesh.devices.reshape(4, 4, 2, 4, 2), ("segment",) + GROUPS)
    return jax.shard_map(
        per_device,
        mesh=fine,
        in_specs=(
            P(None, GROUPS, None),
            P(None, GROUPS, None),
            P("segment", None),
            P("segment", None, None),
            P("segment", None, None),
        ),
        out_specs=(P("segment", None), P("segment", GROUPS, None), P("segment", GROUPS, None)),
        check_vma=False,
    )
```

```python
import functools

import jax
import jax.numpy as jnp
from jax import lax
from jax.experimental import pallas as pl
from jax.experimental.pallas import tpu as pltpu
from jax.sharding import Mesh
from jax.sharding import PartitionSpec as P

eps = 1e-05
bf16 = jnp.bfloat16
f32 = jnp.float32
GROUPS = ("row", "half", "col", "core")
VMEM_BYTES = 8 * 1024 * 1024


def shift(block, axis, distance):
    count = lax.axis_size(axis)
    return lax.ppermute(block, axis, [(j, (j + distance) % count) for j in range(count)])


def swap(block, axis):
    return lax.ppermute(block, axis, [(0, 1), (1, 0)])


def dot(left, right, dims=((1,), (0,))):
    return lax.dot_general(left, right, (dims, ((), ())), preferred_element_type=f32)


def rows_product(left, right):
    return dot(left, right, ((0,), (0,)))


def gather4(block, axis):
    return [block] + [shift(block, axis, 4 - t) for t in (1, 2, 3)]


def from_all(block):
    return [block] + [shift(block, "col", d) for d in (1, 2, 3)]


def pick(array, index, size, axis):
    return lax.dynamic_slice_in_dim(array, index * size, size, axis=axis)


def choose(blocks, index):
    return lax.select_n(index.astype(jnp.int32), *blocks)


def after(arrays, first):
    return list(lax.optimization_barrier(tuple(arrays) + tuple(first)))[: len(arrays)]


def two_parts(array):
    high = lax.reduce_precision(array, 8, 7)
    return high.astype(bf16), (array - high).astype(bf16)


def call(kernel, outs, *operands, places, scratch=()):
    whole = pl.BlockSpec(memory_space=pltpu.VMEM)
    return pl.pallas_call(
        kernel,
        out_shape=[jax.ShapeDtypeStruct(shape, dtype) for shape, dtype in outs],
        in_specs=[pl.BlockSpec(memory_space=pltpu.SMEM)] + [whole] * len(operands),
        out_specs=[whole] * len(outs),
        scratch_shapes=[pltpu.VMEM(shape, dtype) for shape, dtype in scratch],
        compiler_params=pltpu.CompilerParams(vmem_limit_bytes=VMEM_BYTES),
    )(places, *operands)


def silu_of(v):
    return (v / (1.0 + jnp.exp(-v))).astype(bf16)


def slope(v):
    logistic = 1.0 / (1.0 + jnp.exp(-v))
    return logistic * (1.0 + v * (1.0 - logistic))


def as_lanes(column):
    high = column.astype(bf16).astype(f32)
    lane = lax.broadcasted_iota(jnp.int32, (column.shape[0], 128), 1)
    return jnp.where(lane < 64, high, column - high).astype(bf16)


def of_lanes(block):
    return block[:, :1].astype(f32) + block[:, 64:65].astype(f32)


def prep_kernel(places, x_ref, top_ref, up_ref, p0, p1, p2, p3, piece, rms):
    col = places[1]
    for d, out in enumerate((p0, p1, p2, p3)):
        t = lax.rem(col + d, 4)
        for b in range(8):
            lanes = pl.ds(pl.multiple_of(b * 512 + t * 128, 128), 128)
            out[:48, b * 128 : b * 128 + 128] = x_ref[0, :, lanes]
            out[48:, b * 128 : b * 128 + 128] = top_ref[0, :, lanes]
    for b in range(8):
        lanes = pl.ds(pl.multiple_of(b * 512 + col * 128, 128), 128)
        low = (b // 4) * 128
        piece[low : low + 128, (b % 4) * 128 : (b % 4) * 128 + 128] = up_ref[:, lanes]
    squares = jnp.zeros((48, 1), f32)
    for b in range(4):
        wide = x_ref[0, :, b * 1024 : b * 1024 + 1024].astype(f32)
        squares = squares + jnp.sum(wide * wide, axis=-1, keepdims=True)
    rms[...] = as_lanes(lax.rsqrt(squares * (1.0 / 4096.0) + eps))


def prep(places, layer_inputs, top_cotangent, up):
    rows = pl.BlockSpec((1, 48, 4096), lambda g, p: (p[0], 0, 0))
    shapes = [(96, 1024)] * 4 + [(256, 512), (48, 128)]
    return pl.pallas_call(
        prep_kernel,
        grid_spec=pltpu.PrefetchScalarGridSpec(
            num_scalar_prefetch=1,
            grid=(1,),
            in_specs=[rows, rows, pl.BlockSpec((128, 4096), lambda g, p: (p[2], 0))],
            out_specs=[pl.BlockSpec(shape, lambda g, p: (0, 0)) for shape in shapes],
        ),
        out_shape=[jax.ShapeDtypeStruct(shape, bf16) for shape in shapes],
        compiler_params=pltpu.CompilerParams(vmem_limit_bytes=VMEM_BYTES),
    )(places, layer_inputs, top_cotangent, up)


def half_of(weights, part):
    return weights if part is None else weights.at[:, 256 * part : 256 * part + 256]


def grow(places, x_ref, h_ref, mine, other, x_out, sent):
    row, first = places[2], places[3] == 0
    grown = x_ref[...].astype(f32)
    for t in range(4):
        y = lax.rem(row + t, 4)
        h = h_ref[:, pl.ds(pl.multiple_of(y * 128, 128), 128)]
        part = jnp.where(first, mine[t], other[t])
        grown = grown + jnp.concatenate([dot(h, part[:128]), dot(h, part[128:])], 1)
    x_out[...] = grown.astype(bf16)
    wide = x_out[...].astype(f32)
    squares = jnp.sum(wide * wide, axis=-1, keepdims=True)
    total = jnp.zeros((192, 512), f32)
    for t in range(4):
        y = lax.rem(row + t, 4)
        rows = x_out[:, pl.ds(pl.multiple_of(y * 256, 128), 256)]
        total = total + dot(rows, jnp.where(first, other[t], mine[t]))
    sent[:, :512] = total.astype(bf16)
    sent[:, 512:] = as_lanes(squares)


def first_kernel(
    places, b0, b1, b2, b3, x0, x1, x2, x3, mine, other,
    x_start, top, v, r, h, e, x_out, sent,
):
    for j, (b, x) in enumerate(zip((b0, b1, b2, b3), (x0, x1, x2, x3))):
        rows = slice(48 * j, 48 * j + 48)
        x_start[rows, :] = x[:48]
        top[rows, :] = x[48:]
        inverse_rms = of_lanes(b[:, 512:640])
        block = inverse_rms * b[:, :512].astype(f32)
        v[rows, :] = block
        r[rows, :] = jnp.broadcast_to(inverse_rms, (48, 128))
        h[rows, :] = silu_of(block)
        e[rows, :] = b[:, 640:]
    grow(places, x_start, h, mine, other, x_out, sent)


def summed(refs, total, squares=None):
    own = refs[0]
    for j in range(4):
        rows = slice(48 * j, 48 * j + 48)
        value = own[rows, :512].astype(f32)
        if squares is not None:
            column = of_lanes(own[rows, 512:])
        for d in (1, 2, 3):
            low = 48 * ((j - d) % 4)
            value = value + refs[d][low : low + 48, :512].astype(f32)
            if squares is not None:
                column = column + of_lanes(refs[d][low : low + 48, 512:])
        total[rows, :] = value
        if squares is not None:
            squares[rows, :] = jnp.broadcast_to(column, (48, 128))


def normed(refs, v, r):
    summed(refs, v, r)
    r[...] = lax.rsqrt(r[...] * (1.0 / 4096.0) + eps)
    v[...] = r[:, :1] * v[...]


def forward_kernel(part, places, p0, p1, p2, p3, x, mine, other, v, r, h, x_out, sent):
    normed((p0, p1, p2, p3), v, r)
    h[...] = silu_of(v[...])
    grow(places, x, h, half_of(mine, part), half_of(other, part), x_out, sent)


def down_gradient(places, q_out, x, mine, other, acc, gain_sum):
    row, first = places[2], places[3] == 0
    for t in range(4):
        y = lax.rem(row + t, 4)
        lanes = pl.ds(pl.multiple_of(y * 256, 128), 256)
        added = dot(q_out[...], jnp.where(first, other[t], mine[t]), ((1,), (1,)))
        gain_sum[:, lanes] = jnp.sum(added * x[:, lanes].astype(f32), axis=0, keepdims=True)
        if acc is not None:
            acc[:, lanes] = acc[:, lanes] + added


def pass_back(places, e, v, r, g, x, mine, other, q_out, g_out, gain_sum, sent, acc):
    row, first = places[2], places[3] == 0
    contract = ((1,), (1,))
    inverse_rms = r[:, :1]
    value_grad = e[...].astype(f32) * slope(v[...]) * inverse_rms
    q_out[...] = value_grad.astype(bf16)
    pull = inverse_rms * (
        jnp.sum(value_grad * v[...], axis=-1, keepdims=True) * (1.0 / 4096.0)
    )
    acc[...] = g[...].astype(f32) - pull * x[...].astype(f32)
    down_gradient(places, q_out, x, mine, other, acc, gain_sum)
    g_out[...] = acc[...].astype(bf16)
    for t in range(4):
        y = lax.rem(row + t, 4)
        part = jnp.where(first, mine[t], other[t])
        product = dot(g_out[:, :512], part[:128], contract) + dot(
            g_out[:, 512:], part[128:], contract
        )
        sent[:, pl.ds(pl.multiple_of(y * 128, 128), 128)] = product.astype(bf16)


def turn_kernel(
    part, places, p0, p1, p2, p3, e, g, x, mine, other,
    q_out, g_out, gain_sum, sent, h, acc, v, r,
):
    normed((p0, p1, p2, p3), v, r)
    h[...] = silu_of(v[...])
    mine, other = half_of(mine, part), half_of(other, part)
    pass_back(places, e, v, r, g, x, mine, other, q_out, g_out, gain_sum, sent, acc)


def backward_kernel(
    part, places, p0, p1, p2, p3, v, r, g, x, mine, other,
    q_out, g_out, gain_sum, sent, acc, e,
):
    summed((p0, p1, p2, p3), e)
    mine, other = half_of(mine, part), half_of(other, part)
    pass_back(places, e, v, r, g, x, mine, other, q_out, g_out, gain_sum, sent, acc)


def last_kernel(places, p0, p1, p2, p3, v, r, x, mine, other, q_out, gain_sum, e):
    summed((p0, p1, p2, p3), e)
    q_out[...] = (e[...] * slope(v[...]) * r[:, :1]).astype(bf16)
    down_gradient(places, q_out, x, mine, other, None, gain_sum)


def per_device(layer_inputs, top_cotangent, norm_gains, down_weight, up_weight):
    seg = lax.axis_index("segment")
    row = lax.axis_index("row")
    half = lax.axis_index("half")
    col = lax.axis_index("col")
    core = lax.axis_index("core")
    places = jnp.stack([seg, col, row, core]).astype(jnp.int32)
    gain = norm_gains[0]
    down = down_weight[0]
    up = up_weight[0]

    *parts, up_piece, start_rms = prep(places, layer_inputs, top_cotangent, up)

    down_piece = jnp.concatenate(
        [
            lax.dynamic_slice_in_dim(down, ((row * 2 + b) * 4 + col) * 128, 128, axis=0).astype(f32)
            * lax.dynamic_slice_in_dim(gain, ((row * 2 + b) * 4 + col) * 128, 128, axis=0)[:, None]
            for b in (0, 1)
        ],
        0,
    ).astype(bf16)
    scaled = (layer_inputs.astype(f32) * gain).astype(bf16).reshape(192, 4096)
    first = dot(scaled, down).reshape(4, 48, 512).astype(bf16)
    last = dot(top_cotangent.reshape(192, 4096), up, ((1,), (1,))).reshape(4, 48, 512).astype(bf16)
    piece = jnp.where(core == 0, up_piece, down_piece)
    x_blocks = [parts[0]] + [shift(parts[d], "col", d) for d in (1, 2, 3)]
    passed = [first[0]]
    pieces = [piece]
    for d in (1, 2, 3):
        rows = jnp.where(seg == 0, first[d], last[d - 1])
        got = shift(jnp.concatenate([piece, rows], 0), "segment", d)
        passed.append(got[256:])
        pieces.append(got[:256])
    passed.append(last[3])
    pieces = [pieces[0], pieces[3], pieces[2], pieces[1]]
    pieces = after(pieces, x_blocks[1:])
    start = jnp.concatenate(
        [choose(passed[:4], seg), start_rms, choose(passed[1:], seg)], 1
    )
    starts = from_all(start)

    def own_piece(s):
        return choose(pieces, (s + core - seg + 4) % 4)

    blocks = [gather4(own_piece(0), "row")]
    pair = jnp.concatenate([own_piece(1), own_piece(2)], 0)
    blocks.append(gather4(after([pair], blocks[0][1:])[0], "row"))

    wide, narrow = ((192, 1024), bf16), ((192, 512), bf16)
    values = [((192, 512), f32), ((192, 128), f32)]
    mine = jnp.stack(after(blocks[0], starts))
    weights = [(mine, swap(mine, "core"))]
    x_start, top, v, r, h, last_e, x_next, sent = call(
        first_kernel,
        [wide, wide, *values, narrow, narrow, wide, ((192, 640), bf16)],
        *starts, *x_blocks, *weights[0],
        places=places,
    )
    x_rows, hidden, saved = [x_start, x_next], [h], [(v, r)]
    for s in (1, 2):
        got = from_all(sent)
        if s == 1:
            mine = jnp.stack(after(blocks[1], got[1:]))
            weights += [(mine, swap(mine, "core"))] * 2
        else:
            (own,) = after([own_piece(3)], got[1:])
            near = [shift(own, "row", 3), shift(own, "row", 1)]
        v, r, h, x_next, sent = call(
            functools.partial(forward_kernel, s - 1),
            [*values, narrow, wide, ((192, 640), bf16)],
            *got, x_rows[s], *weights[s],
            places=places,
        )
        x_rows.append(x_next)
        hidden.append(h)
        saved.append((v, r))
    got = from_all(sent)
    (own,) = after([own], got[1:] + near)
    far = shift(own, "row", 2)
    got = after(got, [own])

    def down_products(s, q):
        kept = rows_product(x_rows[s], pick(q, core, 256, 1))
        return kept, rows_product(x_rows[s], pick(q, 1 - core, 256, 1)).astype(bf16)

    def up_products(s, g):
        kept = rows_product(hidden[s], pick(g, core, 512, 1))
        return kept, rows_product(hidden[s], pick(g, 1 - core, 512, 1)).astype(bf16)

    def fold(product):
        if product.shape[1] == 256:
            return product.reshape(4, 2, 128, 256)
        lanes = product.reshape(4, 2, 64, 512)
        return jnp.concatenate([lanes[..., :256], lanes[..., 256:]], 2)

    def core_swap(products):
        return swap(jnp.stack([fold(p[1]) for p in products]), "core")

    def core_part(products, got, index):
        kept = [lax.dynamic_index_in_dim(fold(p[0]), index, 1, keepdims=False) for p in products]
        return jnp.stack(kept) + lax.dynamic_index_in_dim(got, index, 2, keepdims=False).astype(f32)

    def at(array, index, axis):
        return lax.dynamic_index_in_dim(array, index, axis, keepdims=False)

    def row_sends(totals):
        return [at(totals, (row + d) % 4, 1).astype(bf16) for d in (1, 2, 3)]

    def row_sums(totals, sends):
        result = at(totals, row, 1)
        for d in (1, 2, 3):
            result = result + shift(sends[d - 1], "row", d).astype(f32)
        return result

    outs = [narrow, wide, ((1, 1024), f32)]
    scratch = [((192, 1024), f32), ((192, 512), f32)]
    q3, g3, t3, sent, h = call(
        functools.partial(turn_kernel, 1),
        [*outs, narrow, narrow],
        *got, last_e, top, x_rows[3], *weights[2],
        places=places, scratch=[scratch[0], *values],
    )
    hidden.append(h)
    got = from_all(sent)
    products_a = [down_products(3, q3), up_products(3, top), up_products(2, g3)]
    mine = jnp.stack(after([own, near[0], far, near[1]], got[1:]))
    weights.append((mine, swap(mine, "core")))
    (core_a,) = after([core_swap(products_a)], got[1:])
    half_a = core_part(products_a, core_a, 1 - half).astype(bf16)
    got = after(got, [half_a])
    q2, g2, t2, sent = call(
        functools.partial(backward_kernel, 0),
        [*outs, narrow],
        *got, *saved[2], g3, x_rows[2], *weights[1],
        places=places, scratch=scratch,
    )
    got = from_all(sent)
    products_b = [down_products(2, q2), up_products(1, g2)]
    (core_b,) = after([core_swap(products_b)], got[1:])
    half_b = core_part(products_b, core_b, 1 - half).astype(bf16)
    got = after(got, [half_b])
    q1, g1, t1, sent = call(
        functools.partial(backward_kernel, None),
        [*outs, narrow],
        *got, *saved[1], g2, x_rows[1], *weights[0],
        places=places, scratch=scratch,
    )
    got = from_all(sent)
    products_c = [down_products(1, q1), up_products(0, g1)]
    from_a, from_b, from_core = after(
        [swap(half_a, "half"), swap(half_b, "half"), core_swap(products_c)], got[1:]
    )
    totals_ab = jnp.concatenate(
        [
            core_part(products_a, core_a, half) + from_a.astype(f32),
            core_part(products_b, core_b, half) + from_b.astype(f32),
        ],
        0,
    )
    sends_ab = row_sends(totals_ab)
    half_c = core_part(products_c, from_core, 1 - half).astype(bf16)
    got = after(got, [*sends_ab, half_c])
    q0, t0 = call(
        last_kernel,
        [narrow, ((1, 1024), f32)],
        *got, *saved[0], x_start, *weights[3],
        places=places, scratch=[((192, 512), f32)],
    )

    sums_ab = row_sums(totals_ab, sends_ab)
    totals_c = core_part(products_c, from_core, half) + swap(half_c, "half").astype(f32)

    gain_sums = jnp.concatenate([t0, t1, t2, t3], 0).reshape(16, 256)

    def with_gain(block, sums):
        high, low = two_parts(sums)
        return jnp.concatenate([block, high, low], 0)

    def gain_of(got):
        return got[:16].astype(f32) + got[16:].astype(f32)

    kept, sent = down_products(0, q0)
    got = swap(with_gain(sent, gain_sums), "core")
    total_d = (kept + got[:1024].astype(f32)).reshape(4, 2, 128, 256)
    gain_sums = gain_sums + gain_of(got[1024:])

    half_d = at(total_d, 1 - half, 1).astype(bf16).reshape(512, 256)
    got = swap(with_gain(half_d, gain_sums), "half")
    total_d = at(total_d, half, 1) + got[:512].astype(f32).reshape(4, 128, 256)
    gain_sums = gain_sums + gain_of(got[512:])
    totals_cd = jnp.concatenate([totals_c, total_d[None]], 0)

    def row_cd(index):
        return at(totals_cd, index, 1).reshape(384, 256)

    sums_cd, gain_next = row_cd(row), gain_sums
    for d in (1, 2, 3):
        sent = with_gain(row_cd((row + d) % 4).astype(bf16), gain_sums)
        got = shift(sent, "row", d)
        sums_cd = sums_cd + got[:384].astype(f32)
        gain_next = gain_next + gain_of(got[384:])
    down_0 = sums_cd[256:]
    gain_sums = gain_next.reshape(4, 4, 256)

    down_3, up_3, up_2, down_2, up_1 = [sums_ab[n] for n in range(5)]
    down_1, up_0 = sums_cd[:128], sums_cd[128:256]
    sections = jnp.stack(
        [
            jnp.concatenate([a, b, gain_sums[s]], 0)
            for s, (a, b) in enumerate(
                ((down_0, up_0), (down_1, up_1), (down_2, up_2), (down_3, up_3))
            )
        ]
    )
    whole = lax.dynamic_index_in_dim(sections, seg, 0, keepdims=False)
    for d in (1, 2, 3):
        part = lax.dynamic_index_in_dim(sections, (seg + d) % 4, 0, keepdims=False)
        high, low = two_parts(part[256:])
        sent = jnp.concatenate([part[:256].astype(bf16), high, low, high, low], 0)
        got = shift(sent, "segment", d).astype(f32)
        whole = whole + jnp.concatenate([got[:256], got[256:260] + got[260:264]], 0)

    down_part = whole[:128]
    up_part = whole[128:256].reshape(2, 4, 2, 8, 256)
    up_mine = lax.dynamic_index_in_dim(up_part, core, 2, keepdims=False).reshape(64, 256)
    up_gone = lax.dynamic_index_in_dim(up_part, 1 - core, 2, keepdims=False).reshape(64, 256)
    kept = jnp.concatenate([pick(down_part, core, 64, 0), up_mine], 0)
    got = swap(jnp.concatenate([pick(down_part, 1 - core, 64, 0), up_gone], 0), "core")
    low = jnp.where(core == 0, kept, got)
    high = jnp.where(core == 0, got, kept)
    product = jnp.concatenate([low[:64], high[:64]], 1)
    quarters = [a.reshape(4, 8, 256) for a in (low[64:96], low[96:], high[64:96], high[96:])]
    up_rows = jnp.concatenate(quarters, 2)
    gain_rows = jnp.broadcast_to(whole[256:].reshape(1, 1, 1024), (4, 8, 1024))
    final = jnp.concatenate([up_rows, gain_rows], 1)

    final_blocks = [lax.dynamic_index_in_dim(final, col, 0, keepdims=False)]
    for t in (1, 2, 3):
        part = lax.dynamic_index_in_dim(final, (col + 4 - t) % 4, 0, keepdims=False)
        final_blocks.append(shift(part, "col", 4 - t))
    ordered = [choose(final_blocks, (t - col + 4) % 4) for t in range(4)]
    final = jnp.concatenate(
        [ordered[t][:, b * 128 : b * 128 + 128] for b in range(8) for t in range(4)], 1
    )
    up_out = final[:8]
    gain_out = final[8:9] / gain[None]
    place = ((row * 2 + half) * 4 + col) * 2 + core
    down_out = product * pick(gain, place, 64, 0)[:, None]
    return gain_out, down_out[None], up_out[None]


def solution(mesh):
    fine = Mesh(mesh.devices.reshape(4, 4, 2, 4, 2), ("segment",) + GROUPS)
    return jax.shard_map(
        per_device,
        mesh=fine,
        in_specs=(
            P(None, GROUPS, None),
            P(None, GROUPS, None),
            P("segment", None),
            P("segment", None, None),
            P("segment", None, None),
        ),
        out_specs=(P("segment", None), P("segment", GROUPS, None), P("segment", GROUPS, None)),
        check_vma=False,
    )
```
